256 devices in a mesh: ctx: 32 (over y, z), tp: 8 (over x, core).
Axes of the slice: x: 4, y: 4, z: 8, core: 2. Of those that a mesh axis runs over, the one named last changes fastest.
Arguments:
- queries: bfloat16 [8192, 2048], P('ctx', 'tp'), may hold values from -8 to 8
- key_states: bfloat16 [8192, 512], P('ctx'), may hold values from -6 to 6
- value_states: bfloat16 [8192, 512], P('ctx'), may hold values from -6 to 6
- saved_output: bfloat16 [8192, 2048], P('ctx', 'tp'), may hold values from -6 to 6
- output_grad: bfloat16 [8192, 2048], P('ctx', 'tp'), may hold values from -6 to 6
- block_place: int32 [32, 2], replicated, may hold values from 0 to 63, as said below
- prompt_length: int32 [1], replicated, may hold values from 128 to 1023
Outputs:
- query_grad: bfloat16 [8192, 2048], P('ctx', 'tp')
- key_grad: bfloat16 [8192, 512], P('ctx')
- value_grad: bfloat16 [8192, 512], P('ctx')
The draws below stay inside these ranges and needn't reach their ends.
Inputs may be any that keep to these rules, and one draw needn't show every extreme that they name: Each of the 2 * 32 blocks appears once; the two blocks of one device lie at mirrored places, block_place[d, 1] = 2 * 32 - 1 - block_place[d, 0], with block_place[d, 0] < 32.
All inputs are finite; a program needn't handle non-finite values.
Results may differ from the reference program's by a relative error of at most 0.012.
Values may be sent and summed in bfloat16 or wider, within the bound.
No kernel may reach another device: no remote copies, remote signals or barrier semaphores. Data moves between devices by JAX's collectives and lax.ppermute only.
A program may use at most 64 MiB of HBM per device.

```python
import jax
import jax.numpy as jnp
from jax import lax

DH = 128
QH = 16
KVH = 4
BLOCK_LEN = 128
SEQ = 8192
N_CTX = 32


def shared_layout(key):
    order = jax.random.permutation(jax.random.fold_in(key, 101), N_CTX).astype(jnp.int32)
    return order


def draw_block_place(key, part):
    order = shared_layout(key)
    return jnp.stack([order, 2 * N_CTX - 1 - order], axis=1).astype(jnp.int32)


def draw_queries(key, part):
    key = jax.random.fold_in(key, 2)
    base = jnp.clip(jax.random.normal(key, (SEQ, QH * DH), jnp.float32), -6.0, 6.0)
    return base.astype(jnp.bfloat16)


def draw_key_states(key, part):
    key = jax.random.fold_in(key, 3)
    base = jnp.clip(jax.random.normal(key, (SEQ, KVH * DH), jnp.float32), -6.0, 6.0)
    return base.astype(jnp.bfloat16)


def block_scale(own_key, shape, pieces, smallest, top_value):
    loudness = 1.0
    for dim, shards_of in pieces:
        steps = jax.random.uniform(jax.random.fold_in(jax.random.fold_in(own_key, 6), dim), (shards_of,), jnp.float32, smallest / len(pieces), top_value / len(pieces))
        loudness = loudness * jnp.repeat(jnp.exp(steps), shape[dim] // shards_of).reshape((-1,) + (1,) * (len(shape) - 1 - dim))
    return loudness


def noise(own_key, dims, width, most, split=(), held_as=jnp.bfloat16):
    values = width * jax.random.normal(own_key, dims, jnp.float32)
    if split:
        values = values * block_scale(own_key, dims, split, -0.22, 0.18)
    return jnp.clip(values, -most, most).astype(held_as)


def setup_inputs(seed: int = 0) -> dict:
    key_of = jax.random.split(jax.random.key(seed), 8)
    return {
        "queries": draw_queries(jax.random.fold_in(key_of[7], 71), 0),
        "key_states": draw_key_states(jax.random.fold_in(key_of[7], 71), 0),
        "value_states": noise(key_of[2], (SEQ, KVH * DH), 1.0, 6.0, ((0, 32),)),
        "saved_output": noise(key_of[3], (SEQ, QH * DH), 1.0, 6.0, ((0, 32), (1, 8))),
        "output_grad": noise(key_of[4], (SEQ, QH * DH), 1.0, 6.0, ((0, 32), (1, 8))),
        "block_place": draw_block_place(jax.random.fold_in(key_of[7], 71), 0),
        "prompt_length": jax.random.randint(key_of[6], (1,), BLOCK_LEN, 8 * BLOCK_LEN).astype(jnp.int32),
    }


def reference(queries, key_states, value_states, saved_output, output_grad, block_place, prompt_length):
    seq_total = queries.shape[0]
    group_size = QH // KVH
    score_scale = DH ** -0.5
    row_ids = jnp.arange(seq_total, dtype=jnp.int32)
    block_table = block_place.reshape(-1)
    where_pos = block_table[row_ids // BLOCK_LEN] * BLOCK_LEN + row_ids % BLOCK_LEN
    prompt_end = prompt_length[0]
    query_span = 2 * BLOCK_LEN
    turn_count = seq_total // query_span
    query_heads = queries.reshape(seq_total, QH, DH)
    grad_heads = output_grad.reshape(seq_total, QH, DH)
    saved_heads = saved_output.reshape(seq_total, QH, DH)
    key_heads = key_states.reshape(seq_total, KVH, DH)
    value_heads = value_states.reshape(seq_total, KVH, DH)

    def one_head(head_index):
        shared = head_index // group_size
        query_one = lax.dynamic_index_in_dim(query_heads, head_index, 1, keepdims=False)
        grad_one = lax.dynamic_index_in_dim(grad_heads, head_index, 1, keepdims=False)
        saved_one = lax.dynamic_index_in_dim(saved_heads, head_index, 1, keepdims=False)
        key_one = lax.dynamic_index_in_dim(key_heads, shared, 1, keepdims=False)
        value_one = lax.dynamic_index_in_dim(value_heads, shared, 1, keepdims=False)

        def query_step(state_pair, turn_index):
            key_acc, value_acc = state_pair
            offset = (turn_index * query_span).astype(jnp.int32)
            query_part = lax.dynamic_slice_in_dim(query_one, offset, query_span, 0)
            grad_part = lax.dynamic_slice_in_dim(grad_one, offset, query_span, 0)
            saved_part = lax.dynamic_slice_in_dim(saved_one, offset, query_span, 0)
            query_pos = lax.dynamic_slice_in_dim(where_pos, offset, query_span, 0)
            scores = jnp.dot(query_part, key_one.T, preferred_element_type=jnp.float32) * score_scale
            visible_mask = (where_pos[None, :] <= query_pos[:, None]) | (where_pos[None, :] < prompt_end)
            scores = jnp.where(visible_mask, scores, -jnp.inf)
            row_peak = jnp.max(scores, axis=1)
            log_total = row_peak + jnp.log(jnp.sum(jnp.exp(scores - row_peak[:, None]), axis=1))
            probs = jnp.exp(scores - log_total[:, None])
            delta = jnp.sum(grad_part.astype(jnp.float32) * saved_part.astype(jnp.float32), axis=1)
            dprobs = jnp.dot(grad_part, value_one.T, preferred_element_type=jnp.float32)
            dscores = (probs * (dprobs - delta[:, None]) * score_scale).astype(jnp.bfloat16)
            query_out = jnp.dot(dscores, key_one, preferred_element_type=jnp.float32)
            key_acc = key_acc + jnp.dot(dscores.T, query_part, preferred_element_type=jnp.float32)
            value_acc = value_acc + jnp.dot(probs.astype(jnp.bfloat16).T, grad_part, preferred_element_type=jnp.float32)
            return (key_acc, value_acc), query_out

        zero_rows = jnp.zeros((seq_total, DH), jnp.float32)
        (key_acc, value_acc), query_out = lax.scan(query_step, (zero_rows, zero_rows), jnp.arange(turn_count, dtype=jnp.int32))
        return query_out.reshape(seq_total, DH), key_acc, value_acc

    query_all, key_all, value_all = lax.map(one_head, jnp.arange(QH, dtype=jnp.int32))
    query_grad = query_all.transpose(1, 0, 2).reshape(seq_total, QH * DH).astype(jnp.bfloat16)
    key_grad = key_all.reshape(KVH, group_size, seq_total, DH).sum(axis=1).transpose(1, 0, 2).reshape(seq_total, KVH * DH).astype(jnp.bfloat16)
    value_grad = value_all.reshape(KVH, group_size, seq_total, DH).sum(axis=1).transpose(1, 0, 2).reshape(seq_total, KVH * DH).astype(jnp.bfloat16)
    return query_grad, key_grad, value_grad
```

```python
import jax
import jax.numpy as jnp
from jax import lax
from jax.experimental import pallas as pl
from jax.experimental.pallas import tpu as pltpu
from jax.sharding import Mesh, PartitionSpec as P

DH = 128
QH = 16
KVH = 4
BLOCK = 128
NY, NZ, NX, NCORE = 4, 8, 4, 2
ROWS = 2 * BLOCK
WIDE = 2 * BLOCK
SCALE = DH ** (-0.5)
EXP2_SCALE = SCALE * 1.4426950408889634
LOWEST = -1e30
VMEM_BYTES = 40 * 1024 * 1024
F32 = jnp.float32
BF16 = jnp.bfloat16


def dot_nt(left, right):
    return lax.dot_general(left, right, (((1,), (1,)), ((), ())), preferred_element_type=F32)


def dot_nn(left, right):
    return lax.dot_general(left, right, (((1,), (0,)), ((), ())), preferred_element_type=F32)


def place_of(place_ref, row, slot):
    return place_ref[row, slot]


def load_keys(core, z_rank, mine_ref, theirs_ref, targets):
    for owner in range(2):

        @pl.when(core == owner)
        def _(owner=owner):
            for j in range(NZ):
                src = lax.rem(z_rank + j, NZ)
                for which, target in targets:
                    target[owner, j] = mine_ref[src, which]
                    target[1 - owner, j] = theirs_ref[src, which]


def load_queries(piece_refs, first_col, target):
    for k, ref in enumerate(piece_refs):
        for slot in range(2):
            for head in range(2):
                target[2 * k + slot, head * BLOCK : (head + 1) * BLOCK, :] = ref[
                    slot * BLOCK : (slot + 1) * BLOCK,
                    first_col + head * DH : first_col + (head + 1) * DH,
                ]


def masked_tiles(place_ref, prompt_ref, y_rank, z_rank, low_places, key_places, tile):
    prompt_end = prompt_ref[0]

    def step(index, carry):
        k = index // NZ
        j = lax.rem(index, NZ)
        query_place = place_of(place_ref, lax.rem(y_rank + NY - k, NY) * NZ + z_rank, 0)
        key_place = place_of(place_ref, y_rank * NZ + lax.rem(z_rank + j, NZ), 0)
        ahead = (key_place > query_place) & (key_place * BLOCK < prompt_end)

        @pl.when(ahead | (index == 0))
        def _():
            tile(2 * k, 0, j, visible_tile(query_place, key_place, prompt_end))

        return carry

    lax.fori_loop(0, NY * NZ, step, 0)
    own_high = place_of(place_ref, y_rank * NZ + z_rank, 1)
    tile(1, 1, 0, visible_tile(own_high, own_high, prompt_end))


def visible_tile(query_place, key_place, prompt_end):
    key_pos = key_place * BLOCK + lax.broadcasted_iota(jnp.int32, (BLOCK, WIDE), 0)
    query_pos = query_place * BLOCK + lax.rem(
        lax.broadcasted_iota(jnp.int32, (BLOCK, WIDE), 1), BLOCK
    )
    return (key_pos <= query_pos) | (key_pos < prompt_end)


def tile_stats(scores):
    groups = scores.reshape(scores.shape[0] // 8, 8, WIDE)
    peak = jnp.max(groups, axis=0)
    total = jnp.sum(jnp.exp2(groups - peak[None]), axis=0)
    return peak, total


def merge_stats(parts):
    peak = parts[0][0]
    for other, _ in parts[1:]:
        peak = jnp.maximum(peak, other)
    total = parts[0][1] * jnp.exp2(parts[0][0] - peak)
    for other, part in parts[1:]:
        total = total + part * jnp.exp2(other - peak)
    return peak, total


def stats_kernel(
    place_ref, prompt_ref, rank_ref, qg0, qg1, qg2, qg3, saved_ref, mine_ref, theirs_ref,
    out_ref, qs, ks, peaks, totals,
):
    y_rank, z_rank, core = rank_ref[0], rank_ref[1], rank_ref[2]
    load_keys(core, z_rank, mine_ref, theirs_ref, [(0, ks)])
    load_queries((qg0, qg1, qg2, qg3), 0, qs)
    low_places = [
        place_of(place_ref, lax.rem(y_rank + NY - k, NY) * NZ + z_rank, 0) for k in range(NY)
    ]
    key_places = [
        place_of(place_ref, y_rank * NZ + lax.rem(z_rank + j, NZ), 0) for j in range(NZ)
    ]
    for k in range(NY):
        high = []
        low = []
        query_high = qs[2 * k + 1]
        for chunk in range(NZ // 2):
            keys = ks[0, 2 * chunk : 2 * chunk + 2].reshape(2 * BLOCK, DH)
            high.append(tile_stats(dot_nt(keys, query_high) * EXP2_SCALE))
        for j in range(NZ):
            if k == 0 and j == 0:
                continue
            slot = jnp.where(key_places[j] < low_places[k], 0, 1)
            peak, total = tile_stats(dot_nt(ks[slot, j], qs[2 * k + slot]) * EXP2_SCALE)
            high.append((jnp.where(slot == 1, peak, LOWEST), jnp.where(slot == 1, total, 0.0)))
            low.append((jnp.where(slot == 0, peak, LOWEST), jnp.where(slot == 0, total, 0.0)))
        for slot, parts in ((0, low), (1, high)):
            peak, total = merge_stats(parts)
            peaks[2 * k + slot] = peak
            totals[2 * k + slot] = total

    def tile(query_index, slot, j, visible):
        scores = dot_nt(ks[slot, j], qs[query_index]) * EXP2_SCALE
        peak, total = tile_stats(jnp.where(visible, scores, LOWEST))
        total = jnp.where(peak > 0.5 * LOWEST, total, 0.0)
        peak, total = merge_stats([(peaks[query_index], totals[query_index]), (peak, total)])
        peaks[query_index] = peak
        totals[query_index] = total

    masked_tiles(place_ref, prompt_ref, y_rank, z_rank, low_places, key_places, tile)

    for k in range(NY):
        for slot in range(2):
            peak = peaks[2 * k + slot]
            top = jnp.max(peak, axis=0, keepdims=True)
            total = jnp.sum(totals[2 * k + slot] * jnp.exp2(peak - top), axis=0, keepdims=True)
            row = lax.rem(y_rank + NY - k, NY) * 2 + slot
            out_ref[pl.ds(row, 1), :] = top
            out_ref[pl.ds(row + 8, 1), :] = total
    out_ref[16:24, :] = jnp.zeros((8, WIDE), F32)
    for slot in range(2):
        for head in range(2):
            rows = slice(slot * BLOCK, (slot + 1) * BLOCK)
            grad = qg0[rows, WIDE + head * DH : WIDE + (head + 1) * DH].astype(F32)
            saved = saved_ref[rows, head * DH : (head + 1) * DH].astype(F32)
            out_ref[16 + slot : 17 + slot, head * BLOCK : (head + 1) * BLOCK] = jnp.sum(
                (grad * saved).T, axis=0, keepdims=True
            )


def grad_kernel(
    place_ref, prompt_ref, rank_ref, qg0, qg1, qg2, qg3, mine_ref, theirs_ref, st0, st1, st2, st3,
    own_query, query1, query2, query3, keep_ref, send_ref,
    qs, gs, ks, vs, kt, lse, delta, lse_rows, query_acc, key_acc, value_acc,
):
    y_rank, z_rank, core = rank_ref[0], rank_ref[1], rank_ref[2]
    load_keys(core, z_rank, mine_ref, theirs_ref, [(0, ks), (1, vs)])
    load_queries((qg0, qg1, qg2, qg3), 0, qs)
    load_queries((qg0, qg1, qg2, qg3), WIDE, gs)
    for slot in range(2):
        for j in range(NZ):
            kt[slot, :, j * BLOCK : (j + 1) * BLOCK] = ks[slot, j].T
    stats = (st0, st1, st2, st3)
    top, total = merge_stats([(ref[0:8, :], ref[8:16, :]) for ref in stats])
    lse_rows[...] = top + jnp.log2(total)
    for k in range(NY):
        for slot in range(2):
            row = lax.rem(y_rank + NY - k, NY) * 2 + slot
            lse[2 * k + slot] = jnp.broadcast_to(lse_rows[pl.ds(row, 1), :], (8, WIDE))
            delta[2 * k + slot] = jnp.broadcast_to(stats[k][16 + slot : 17 + slot, :], (8, WIDE))

    def tile_grads(query_index, keys, values, visible=None):
        length = keys.shape[0]
        shape = (length // 8, 8, WIDE)
        scores = (dot_nt(keys, qs[query_index]) * EXP2_SCALE).reshape(shape)
        logits = scores - lse[query_index][None]
        if visible is not None:
            logits = jnp.where(visible.reshape(shape), logits, LOWEST)
        probs = jnp.exp2(logits)
        dprobs = dot_nt(values, gs[query_index]).reshape(shape)
        dscores = (probs * (dprobs - delta[query_index][None])).reshape(length, WIDE)
        return probs.reshape(length, WIDE).astype(BF16), dscores.astype(BF16)

    for chunk in range(NZ // 2):
        blocks = slice(2 * chunk, 2 * chunk + 2)
        columns = slice(2 * chunk * BLOCK, (2 * chunk + 2) * BLOCK)
        keys = ks[0, blocks].reshape(2 * BLOCK, DH)
        values = vs[0, blocks].reshape(2 * BLOCK, DH)
        key_sum = None
        for k in range(NY):
            probs, dscores = tile_grads(2 * k + 1, keys, values)
            value_part = dot_nn(probs, gs[2 * k + 1])
            key_part = dot_nn(dscores, qs[2 * k + 1])
            if key_sum is None:
                key_sum, value_sum = key_part, value_part
            else:
                key_sum, value_sum = key_sum + key_part, value_sum + value_part
            query_part = dot_nn(kt[0, :, columns], dscores)
            if chunk == 0:
                query_acc[2 * k + 1] = query_part
            else:
                query_acc[2 * k + 1] += query_part
        key_acc[0, blocks] = key_sum.reshape(2, BLOCK, DH)
        value_acc[0, blocks] = value_sum.reshape(2, BLOCK, DH)
    for k in range(NY):
        query_acc[2 * k] = jnp.zeros((DH, WIDE), F32)
    key_acc[1] = jnp.zeros((NZ, BLOCK, DH), F32)
    value_acc[1] = jnp.zeros((NZ, BLOCK, DH), F32)

    def add_tile(query_index, slot, j, columns, visible=None):
        probs, dscores = tile_grads(query_index, ks[slot, j], vs[slot, j], visible)
        value_acc[slot, j] += dot_nn(probs, gs[query_index])
        key_acc[slot, j] += dot_nn(dscores, qs[query_index])
        query_acc[query_index] += dot_nn(kt[slot, :, columns], dscores)

    low_places = [
        place_of(place_ref, lax.rem(y_rank + NY - k, NY) * NZ + z_rank, 0) for k in range(NY)
    ]
    key_places = [
        place_of(place_ref, y_rank * NZ + lax.rem(z_rank + j, NZ), 0) for j in range(NZ)
    ]
    for j in range(NZ):
        for k in range(NY):
            if k == 0 and j == 0:
                continue
            slot = jnp.where(key_places[j] < low_places[k], 0, 1)
            add_tile(2 * k + slot, slot, j, slice(j * BLOCK, (j + 1) * BLOCK))

    def masked_tile(query_index, slot, j, visible):
        first = j * BLOCK
        if not isinstance(first, int):
            first = pl.multiple_of(first, BLOCK)
        add_tile(query_index, slot, j, pl.ds(first, BLOCK), visible)

    masked_tiles(place_ref, prompt_ref, y_rank, z_rank, low_places, key_places, masked_tile)

    for k, out in enumerate((own_query, query1, query2, query3)):
        for slot in range(2):
            for head in range(2):
                block = query_acc[2 * k + slot, :, head * BLOCK : (head + 1) * BLOCK].T * SCALE
                out[
                    slot * BLOCK : (slot + 1) * BLOCK, head * DH : (head + 1) * DH
                ] = block.astype(out.dtype)
    for owner in range(2):

        @pl.when(core == owner)
        def _(owner=owner):
            for j in range(NZ):
                to = lax.rem(z_rank + j, NZ)
                for slot in range(2):
                    rows = slice(slot * BLOCK, (slot + 1) * BLOCK)
                    key_block = key_acc[slot, j] * SCALE
                    value_block = value_acc[slot, j]
                    kept, sent = (key_block, value_block) if owner == 0 else (value_block, key_block)
                    keep_ref[to, rows, :] = kept
                    send_ref[to, rows, :] = sent.astype(BF16)


def join_kernel(rank_ref, own_ref, p1, p2, p3, theirs_ref, key_ref, value_ref):
    x_rank, core = rank_ref[3], rank_ref[2]
    for k, ref in enumerate((own_ref, p1, p2, p3)):
        column = pl.multiple_of(lax.rem(x_rank + NX - k, NX) * DH, DH)
        for owner in range(2):

            @pl.when(core == owner)
            def _(owner=owner, ref=ref, k=k, column=column):
                outs = (key_ref, value_ref)
                outs[owner][:, pl.ds(column, DH)] = ref[...]
                outs[1 - owner][:, pl.ds(column, DH)] = theirs_ref[k]


def call(kernel, n_scalars, n_arrays, out_shape, scratch=(), flops=0):
    return pl.pallas_call(
        kernel,
        out_shape=out_shape,
        in_specs=[pl.BlockSpec(memory_space=pltpu.SMEM)] * n_scalars
        + [pl.BlockSpec(memory_space=pltpu.VMEM)] * n_arrays,
        out_specs=jax.tree.map(lambda _: pl.BlockSpec(memory_space=pltpu.VMEM), out_shape),
        scratch_shapes=list(scratch),
        compiler_params=pltpu.CompilerParams(vmem_limit_bytes=VMEM_BYTES),
        cost_estimate=pl.CostEstimate(flops=flops, bytes_accessed=4 << 20, transcendentals=0),
    )


def shifts(array, axis, size):
    return [
        lax.ppermute(array, axis, [(i, (i + k) % size) for i in range(size)])
        for k in range(1, size)
    ]


def shards(
    queries, key_states, value_states, saved_output, output_grad, block_place, prompt_length
):
    y_rank, z_rank = lax.axis_index("y"), lax.axis_index("z")
    x_rank, core = lax.axis_index("x"), lax.axis_index("core")
    ranks = jnp.stack([y_rank, z_rank, core, x_rank]).astype(jnp.int32)
    swap = [(0, 1), (1, 0)]

    with jax.named_scope("gather_queries"):
        own_qg = jnp.concatenate([queries, output_grad], axis=1)
        pieces = [own_qg] + shifts(own_qg, "y", NY)
    with jax.named_scope("gather_keys"):
        start = (core * BLOCK, x_rank * DH)
        own_kv = jnp.stack(
            [
                lax.dynamic_slice(key_states, start, (BLOCK, DH)),
                lax.dynamic_slice(value_states, start, (BLOCK, DH)),
            ]
        )
        spread = jnp.broadcast_to(own_kv[None], (NZ, 2, BLOCK, DH))
        mine = lax.all_to_all(spread, "z", 0, 0, tiled=True)
        theirs = lax.ppermute(mine, "core", swap)
    with jax.named_scope("stats"):
        stats = call(
            stats_kernel, 3, 7, jax.ShapeDtypeStruct((24, WIDE), F32),
            [
                pltpu.VMEM((8, WIDE, DH), BF16),
                pltpu.VMEM((2, NZ, BLOCK, DH), BF16),
                pltpu.VMEM((8, 8, WIDE), F32),
                pltpu.VMEM((8, 8, WIDE), F32),
            ],
            flops=600_000_000,
        )(block_place, prompt_length, ranks, *pieces, saved_output, mine, theirs)
        all_stats = [stats] + shifts(stats, "y", NY)
    with jax.named_scope("grads"):
        piece = jax.ShapeDtypeStruct((ROWS, WIDE), BF16)
        own_query, query1, query2, query3, keep, send = call(
            grad_kernel, 3, 10,
            (
                jax.ShapeDtypeStruct((ROWS, WIDE), F32), piece, piece, piece,
                jax.ShapeDtypeStruct((NZ, ROWS, DH), F32),
                jax.ShapeDtypeStruct((NZ, ROWS, DH), BF16),
            ),
            [
                pltpu.VMEM((8, WIDE, DH), BF16),
                pltpu.VMEM((8, WIDE, DH), BF16),
                pltpu.VMEM((2, NZ, BLOCK, DH), BF16),
                pltpu.VMEM((2, NZ, BLOCK, DH), BF16),
                pltpu.VMEM((2, DH, NZ * BLOCK), BF16),
                pltpu.VMEM((8, 8, WIDE), F32),
                pltpu.VMEM((8, 8, WIDE), F32),
                pltpu.VMEM((8, WIDE), F32),
                pltpu.VMEM((8, DH, WIDE), F32),
                pltpu.VMEM((2, NZ, BLOCK, DH), F32),
                pltpu.VMEM((2, NZ, BLOCK, DH), F32),
            ],
            flops=3_000_000_000,
        )(block_place, prompt_length, ranks, *pieces, mine, theirs, *all_stats)
    with jax.named_scope("query_sum"):
        back = [
            lax.ppermute(part, "y", [(i, (i - k) % NY) for i in range(NY)])
            for k, part in ((1, query1), (2, query2), (3, query3))
        ]
        query_grad = own_query
        for part in back:
            query_grad = query_grad + part.astype(F32)
        query_grad = query_grad.astype(BF16)
    with jax.named_scope("key_sum"):
        pair = (keep + lax.ppermute(send, "core", swap).astype(F32)).astype(BF16)
        terms = lax.all_to_all(pair, "z", 0, 0, tiled=True)
        own_sum = jnp.sum(terms.astype(F32), axis=0).astype(BF16)
    with jax.named_scope("heads"):
        heads = shifts(own_sum, "x", NX)
        theirs_sum = lax.ppermute(jnp.stack([own_sum, *heads]), "core", swap)
        full = jax.ShapeDtypeStruct((ROWS, KVH * DH), BF16)
        key_grad, value_grad = call(join_kernel, 1, 5, (full, full))(
            ranks, own_sum, *heads, theirs_sum
        )
    return (query_grad, key_grad, value_grad)


def solution(mesh):
    grid = Mesh(mesh.devices.reshape(NY, NZ, NX, NCORE), ("y", "z", "x", "core"))
    rows, heads = ("y", "z"), ("x", "core")
    placed = (
        P(rows, heads),
        P(rows, None),
        P(rows, None),
        P(rows, heads),
        P(rows, heads),
        P(),
        P(),
    )
    return jax.shard_map(
        shards,
        mesh=grid,
        in_specs=placed,
        out_specs=(P(rows, heads), P(rows, None), P(rows, None)),
        check_vma=False,
    )
```

```python
import functools

import jax
import jax.numpy as jnp
from jax import lax
from jax.experimental import pallas as pl
from jax.experimental.pallas import tpu as pltpu
from jax.sharding import Mesh, PartitionSpec as P

DH = 128
QH = 16
KVH = 4
BLOCK = 128
NY, NZ, NX, NCORE = 4, 8, 4, 2
ROWS = 2 * BLOCK
WIDE = 2 * BLOCK
PACKED = ROWS + 16
SCALE = DH ** (-0.5)
EXP2_SCALE = SCALE * 1.4426950408889634
LOWEST = -1e30
VMEM_BYTES = 24 * 1024 * 1024
WHOLE_VMEM = 60 * 1024 * 1024
F32 = jnp.float32
BF16 = jnp.bfloat16


def dot_nt(left, right):
    return lax.dot_general(left, right, (((1,), (1,)), ((), ())), preferred_element_type=F32)


def dot_nn(left, right):
    return lax.dot_general(left, right, (((1,), (0,)), ((), ())), preferred_element_type=F32)


def load_keys(core, z_rank, mine_ref, theirs_ref, which, target):
    for owner in range(2):

        @pl.when(core == owner)
        def _(owner=owner):
            for j in range(NZ):
                src = lax.rem(z_rank + j, NZ)
                target[owner, j] = mine_ref[src, which]
                target[1 - owner, j] = theirs_ref[src, which]


def load_queries(core, piece_refs, first_col, target, delta=None):
    def load(k, ref, first_col):
        for slot in range(2):
            for head in range(2):
                target[2 * k + slot, head * BLOCK : (head + 1) * BLOCK, :] = ref[
                    slot * BLOCK : (slot + 1) * BLOCK,
                    first_col + head * DH : first_col + (head + 1) * DH,
                ]
        if delta is not None and k:
            lines = ref[ROWS:PACKED, :WIDE].astype(F32)
            for slot in range(2):
                line = sum(lines[3 * slot + i : 3 * slot + i + 1, :] for i in range(3))
                delta[2 * k + slot] = jnp.broadcast_to(line, (8, WIDE))

    load(0, piece_refs[0], 0)
    load(1, piece_refs[1], first_col)
    load(3, piece_refs[3], first_col)
    for owner, ref in ((0, piece_refs[2]), (1, piece_refs[4])):

        @pl.when(core == owner)
        def _(ref=ref):
            load(2, ref, first_col)


def visible_tile(query_place, key_place, prompt_end):
    key_pos = key_place * BLOCK + lax.broadcasted_iota(jnp.int32, (BLOCK, WIDE), 0)
    query_pos = query_place * BLOCK + lax.rem(
        lax.broadcasted_iota(jnp.int32, (BLOCK, WIDE), 1), BLOCK
    )
    return (key_pos <= query_pos) | (key_pos < prompt_end)


def tile_max(scores):
    return jnp.max(scores.reshape(scores.shape[0] // 8, 8, WIDE), axis=0)


def tile_sum(probs):
    return jnp.sum(probs.reshape(probs.shape[0] // 8, 8, WIDE), axis=0)


def all_places(place_ref, y_rank, z_rank):
    low_places = [
        place_ref[0, lax.rem(y_rank + NY - k, NY) * NZ + z_rank] for k in range(NY)
    ]
    key_places = [place_ref[0, y_rank * NZ + lax.rem(z_rank + j, NZ)] for j in range(NZ)]
    return low_places, key_places


def extra_tile(low_places, key_places, prompt_end, k, j):
    ahead = (key_places[j] > low_places[k]) & (key_places[j] * BLOCK < prompt_end)
    return (ahead | (key_places[j] == low_places[k])) if (k, j) == (0, 0) else ahead


def probs_kernel(
    place_ref, prompt_ref, q0, q1, q2, q3, q4, mine_ref, theirs_ref,
    qs, ks, dense_ref, pair_ref, extra_ref, stats_ref, dense, pair, extra, low_peak,
):
    y_rank, z_rank, core = (lax.axis_index(axis) for axis in ("y", "z", "core"))
    prompt_end = prompt_ref[0]
    load_keys(core, z_rank, mine_ref, theirs_ref, 0, ks)
    load_queries(core, (q0, q1, q2, q3, q4), 0, qs)
    low_places, key_places = all_places(place_ref, y_rank, z_rank)
    own_high = place_ref[1, y_rank * NZ + z_rank]
    stats_ref[...] = jnp.zeros((24, WIDE), F32)
    for k in range(NY):
        query_high = qs[2 * k + 1]
        high = []
        low = []
        for chunk in range(NZ // 2):
            keys = ks[0, 2 * chunk : 2 * chunk + 2].reshape(2 * BLOCK, DH)
            scores = dot_nt(keys, query_high) * EXP2_SCALE
            dense[2 * chunk * BLOCK : 2 * (chunk + 1) * BLOCK, :] = scores
            high.append(tile_max(scores))
        for j in range(NZ):
            is_low = key_places[j] < low_places[k]
            slot = jnp.where(is_low, 0, 1)
            scores = dot_nt(ks[slot, j], qs[2 * k + slot]) * EXP2_SCALE
            if (k, j) == (0, 0):
                scores = jnp.where(visible_tile(own_high, own_high, prompt_end), scores, LOWEST)
            pair[j * BLOCK : (j + 1) * BLOCK, :] = scores
            peak = tile_max(scores)
            high.append(jnp.where(is_low, LOWEST, peak))
            low.append(jnp.where(is_low, peak, LOWEST))
        low_peak[...] = functools.reduce(jnp.maximum, low)
        for j in range(NZ):

            @pl.when(extra_tile(low_places, key_places, prompt_end, k, j))
            def _(k=k, j=j):
                scores = dot_nt(ks[0, j], qs[2 * k]) * EXP2_SCALE
                visible = visible_tile(low_places[k], key_places[j], prompt_end)
                scores = jnp.where(visible, scores, LOWEST)
                extra[j] = scores
                low_peak[...] = jnp.maximum(low_peak[...], tile_max(scores))

        high_top = jnp.max(functools.reduce(jnp.maximum, high), axis=0, keepdims=True)
        low_top = jnp.max(low_peak[...], axis=0, keepdims=True)
        high_sum = jnp.zeros((8, WIDE), F32)
        low_sum = jnp.zeros((8, WIDE), F32)
        for chunk in range(NZ // 2):
            rows = slice(2 * chunk * BLOCK, 2 * (chunk + 1) * BLOCK)
            probs = jnp.exp2(dense[rows, :] - high_top)
            dense_ref[k, rows, :] = probs.astype(BF16)
            high_sum = high_sum + tile_sum(probs)
        for j in range(NZ):
            rows = slice(j * BLOCK, (j + 1) * BLOCK)
            is_low = key_places[j] < low_places[k]
            probs = jnp.exp2(pair[rows, :] - jnp.where(is_low, low_top, high_top))
            pair_ref[k, rows, :] = probs.astype(BF16)
            part = tile_sum(probs)
            high_sum = high_sum + jnp.where(is_low, 0.0, part)
            low_sum = low_sum + jnp.where(is_low, part, 0.0)
        low_peak[...] = low_sum
        for j in range(NZ):

            @pl.when(extra_tile(low_places, key_places, prompt_end, k, j))
            def _(k=k, j=j):
                probs = jnp.exp2(extra[j] - low_top)
                extra_ref[k, j] = probs.astype(BF16)
                low_peak[...] += tile_sum(probs)

        row = lax.rem(y_rank + NY - k, NY) * 2
        low_total = jnp.sum(low_peak[...], axis=0, keepdims=True)
        high_total = jnp.sum(high_sum, axis=0, keepdims=True)
        stats_ref[pl.ds(row, 1), :] = low_top
        stats_ref[pl.ds(row + 1, 1), :] = high_top
        stats_ref[pl.ds(row + 8, 1), :] = low_total
        stats_ref[pl.ds(row + 9, 1), :] = high_total


def scores_kernel(
    place_ref, prompt_ref, ks, g0, g1, g2, g3, g4, own_delta, mine_ref, theirs_ref,
    dense_ref, pair_ref, extra_ref,
    gs, dense_out, pair_out, extra_out, query_acc, vs, kt, delta,
):
    y_rank, z_rank, core = (lax.axis_index(axis) for axis in ("y", "z", "core"))
    prompt_end = prompt_ref[0]
    load_keys(core, z_rank, mine_ref, theirs_ref, 1, vs)
    load_queries(core, (g0, g1, g2, g3, g4), WIDE, gs, delta)
    for slot in range(2):
        delta[slot] = jnp.broadcast_to(own_delta[slot : slot + 1, :], (8, WIDE))
    low_places, key_places = all_places(place_ref, y_rank, z_rank)
    for slot in range(2):
        for j in range(NZ):
            kt[slot, :, j * BLOCK : (j + 1) * BLOCK] = ks[slot, j].T

    def scores(probs, values, query_index):
        length = values.shape[0]
        shape = (length // 8, 8, WIDE)
        dprobs = dot_nt(values, gs[query_index]).reshape(shape) - delta[query_index][None]
        return (probs.astype(F32) * dprobs.reshape(length, WIDE)).astype(BF16)

    for k in range(NY):
        for chunk in range(NZ // 2):
            rows = slice(2 * chunk * BLOCK, 2 * (chunk + 1) * BLOCK)
            values = vs[0, 2 * chunk : 2 * chunk + 2].reshape(2 * BLOCK, DH)
            dense_out[k, rows, :] = scores(dense_ref[k, rows, :], values, 2 * k + 1)
        query_acc[2 * k + 1] = dot_nn(kt[0], dense_out[k])
        query_acc[2 * k] = jnp.zeros((DH, WIDE), F32)
        for j in range(NZ):
            rows = slice(j * BLOCK, (j + 1) * BLOCK)
            slot = jnp.where(key_places[j] < low_places[k], 0, 1)
            dscores = scores(pair_ref[k, rows, :], vs[slot, j], 2 * k + slot)
            pair_out[k, rows, :] = dscores
            query_acc[2 * k + slot] += dot_nn(kt[slot, :, rows], dscores)
        for j in range(NZ):

            @pl.when(extra_tile(low_places, key_places, prompt_end, k, j))
            def _(k=k, j=j):
                dscores = scores(extra_ref[k, j], vs[0, j], 2 * k)
                extra_out[k, j] = dscores
                query_acc[2 * k] += dot_nn(kt[0, :, j * BLOCK : (j + 1) * BLOCK], dscores)


def grad_kernel(
    place_ref, prompt_ref, qs, gs, dense_p, pair_p, extra_p, dense_s, pair_s, extra_s,
    query_acc, st0, st1, st2, st3,
    own_query, query1, query2, query3, keep_ref, send_ref,
    qr, gr, factor_rows, key_acc, value_acc,
):
    y_rank, z_rank, core = (lax.axis_index(axis) for axis in ("y", "z", "core"))
    prompt_end = prompt_ref[0]
    low_places, key_places = all_places(place_ref, y_rank, z_rank)
    parts = [(ref[0:8, :], ref[8:16, :]) for ref in (st0, st1, st2, st3)]
    top = functools.reduce(jnp.maximum, [peak for peak, _ in parts])
    total = sum(part * jnp.exp2(peak - top) for peak, part in parts)
    factor_rows[...] = jnp.exp2(parts[0][0] - top) / total
    for k in range(NY):
        for slot in range(2):
            row = lax.rem(y_rank + NY - k, NY) * 2 + slot
            line = factor_rows[pl.ds(row, 1), :]
            column = jnp.broadcast_to(line, (BLOCK, WIDE)).T
            index = 2 * k + slot
            qr[index] = (qs[index].astype(F32) * column).astype(BF16)
            gr[index] = (gs[index].astype(F32) * column).astype(BF16)
            out = (own_query, query1, query2, query3)[k]
            for head in range(2):
                lanes = slice(head * BLOCK, (head + 1) * BLOCK)
                block = (query_acc[index, :, lanes] * (line[:, lanes] * SCALE)).T
                out[
                    slot * BLOCK : (slot + 1) * BLOCK, head * DH : (head + 1) * DH
                ] = block.astype(out.dtype)
    for chunk in range(NZ // 2):
        blocks = slice(2 * chunk, 2 * chunk + 2)
        rows = slice(2 * chunk * BLOCK, 2 * (chunk + 1) * BLOCK)
        key_sum = value_sum = None
        for k in range(NY):
            value_part = dot_nn(dense_p[k, rows, :], gr[2 * k + 1])
            key_part = dot_nn(dense_s[k, rows, :], qr[2 * k + 1])
            value_sum = value_part if k == 0 else value_sum + value_part
            key_sum = key_part if k == 0 else key_sum + key_part
        key_acc[0, blocks] = key_sum.reshape(2, BLOCK, DH)
        value_acc[0, blocks] = value_sum.reshape(2, BLOCK, DH)
    key_acc[1] = jnp.zeros((NZ, BLOCK, DH), F32)
    value_acc[1] = jnp.zeros((NZ, BLOCK, DH), F32)
    for j in range(NZ):
        rows = slice(j * BLOCK, (j + 1) * BLOCK)
        for k in range(NY):
            slot = jnp.where(key_places[j] < low_places[k], 0, 1)
            value_acc[slot, j] += dot_nn(pair_p[k, rows, :], gr[2 * k + slot])
            key_acc[slot, j] += dot_nn(pair_s[k, rows, :], qr[2 * k + slot])
    for j in range(NZ):
        for k in range(NY):

            @pl.when(extra_tile(low_places, key_places, prompt_end, k, j))
            def _(k=k, j=j):
                value_acc[0, j] += dot_nn(extra_p[k, j], gr[2 * k])
                key_acc[0, j] += dot_nn(extra_s[k, j], qr[2 * k])

    for owner in range(2):

        @pl.when(core == owner)
        def _(owner=owner):
            for j in range(NZ):
                to = lax.rem(z_rank + j, NZ)
                for slot in range(2):
                    rows = slice(slot * BLOCK, (slot + 1) * BLOCK)
                    key_block = key_acc[slot, j] * SCALE
                    value_block = value_acc[slot, j]
                    kept, sent = (key_block, value_block) if owner == 0 else (value_block, key_block)
                    keep_ref[to, rows, :] = kept
                    send_ref[to, rows, :] = sent.astype(BF16)


def prepare_kernel(
    queries_ref, saved_ref, grad_ref, key_ref, value_ref, out_ref, spread_ref, delta_ref,
    saved, sems,
):
    first_row = pl.multiple_of(lax.axis_index("core") * BLOCK, BLOCK)
    first_col = pl.multiple_of(lax.axis_index("x") * DH, DH)
    own = (pl.ds(first_row, BLOCK), pl.ds(first_col, DH))
    copies = [
        pltpu.make_async_copy(source, target, sems.at[i])
        for i, (source, target) in enumerate(
            (
                (key_ref.at[own], spread_ref.at[0, 0]),
                (value_ref.at[own], spread_ref.at[0, 1]),
                (grad_ref, out_ref.at[pl.ds(0, ROWS), pl.ds(WIDE, WIDE)]),
                (saved_ref, saved),
                (queries_ref, out_ref.at[pl.ds(0, ROWS), pl.ds(0, WIDE)]),
            )
        )
    ]
    for copy in copies:
        copy.start()
    copies[0].wait()
    copies[1].wait()
    for z in range(1, NZ):
        spread_ref[z] = spread_ref[0]
    copies[2].wait()
    copies[3].wait()
    lines = []
    for slot in range(2):
        rows = slice(slot * BLOCK, (slot + 1) * BLOCK)
        heads = []
        for head in range(2):
            columns = slice(head * DH, (head + 1) * DH)
            beside = slice(WIDE + head * DH, WIDE + (head + 1) * DH)
            product = out_ref[rows, beside].astype(F32) * saved[rows, columns].astype(F32)
            heads.append(jnp.sum(product.T, axis=0, keepdims=True))
        rest = jnp.concatenate(heads, axis=1)
        for _ in range(3):
            term = rest.astype(BF16).astype(F32)
            lines.append(term)
            rest = rest - term
        delta_ref[slot : slot + 1, :] = jnp.concatenate(heads, axis=1)
    lines.append(jnp.zeros((PACKED - ROWS - len(lines), WIDE), F32))
    out_ref[ROWS:, :WIDE] = jnp.concatenate(lines, axis=0).astype(BF16)
    out_ref[ROWS:, WIDE:] = jnp.zeros((PACKED - ROWS, WIDE), BF16)
    copies[4].wait()


def join_kernel(own_ref, p1, p2, p3, theirs_ref, key_ref, value_ref):
    x_rank, core = lax.axis_index("x"), lax.axis_index("core")
    for k, ref in enumerate((own_ref, p1, p2, p3)):
        column = pl.multiple_of(lax.rem(x_rank + NX - k, NX) * DH, DH)
        for owner in range(2):

            @pl.when(core == owner)
            def _(owner=owner, ref=ref, k=k, column=column):
                outs = (key_ref, value_ref)
                outs[owner][:, pl.ds(column, DH)] = ref[...]
                outs[1 - owner][:, pl.ds(column, DH)] = theirs_ref[k]


def call(kernel, n_scalars, n_arrays, out_shape, scratch=(), flops=0, far_in=0):
    return pl.pallas_call(
        kernel,
        out_shape=out_shape,
        in_specs=[pl.BlockSpec(memory_space=pltpu.SMEM)] * n_scalars
        + [pl.BlockSpec(memory_space=pl.ANY)] * far_in
        + [pl.BlockSpec(memory_space=pltpu.VMEM)] * n_arrays,
        out_specs=jax.tree.map(lambda _: pl.BlockSpec(memory_space=pltpu.VMEM), out_shape),
        scratch_shapes=list(scratch),
        compiler_params=pltpu.CompilerParams(vmem_limit_bytes=WHOLE_VMEM if far_in else VMEM_BYTES),
        cost_estimate=pl.CostEstimate(flops=flops, bytes_accessed=0, transcendentals=0),
    )


def shifts(array, axis, size):
    return [
        lax.ppermute(array, axis, [(i, (i + k) % size) for i in range(size)])
        for k in range(1, size)
    ]


def step_of_one_core(mover, step):
    return [
        (y * NCORE + core, (y + step) % NY * NCORE + core if core == mover else y * NCORE + core)
        for y in range(NY)
        for core in range(NCORE)
    ]


def shards(
    queries, key_states, value_states, saved_output, output_grad, block_place, prompt_length
):
    scalars = (block_place.T, prompt_length)
    shape = jax.ShapeDtypeStruct

    def swap(array):
        return lax.ppermute(array, "core", [(0, 1), (1, 0)])

    blocks = shape((8, WIDE, DH), BF16)
    sides = shape((2, NZ, BLOCK, DH), BF16)
    tall = shape((NY, NZ * BLOCK, WIDE), BF16)
    tiles = shape((NY, NZ, BLOCK, WIDE), BF16)
    with jax.named_scope("gather"):
        packed, spread, own_delta = call(
            prepare_kernel, 0, 0,
            (
                shape((PACKED, 2 * WIDE), BF16), shape((NZ, 2, BLOCK, DH), BF16),
                shape((8, WIDE), F32),
            ),
            [pltpu.VMEM((ROWS, WIDE), BF16), pltpu.SemaphoreType.DMA((5,))],
            far_in=5,
        )(queries, saved_output, output_grad, key_states, value_states)
        down = lax.ppermute(packed, "y", [(i, (i - 1) % NY) for i in range(NY)])
        up = lax.ppermute(packed, "y", [(i, (i + 1) % NY) for i in range(NY)])
        far = lax.ppermute(packed, ("y", "core"), step_of_one_core(0, 2))
        relayed = lax.ppermute(down, ("y", "core"), step_of_one_core(1, -1))
        pieces = [up, far, down, relayed]
        mine = lax.all_to_all(spread, "z", 0, 0, tiled=True)
        mine, *pieces = lax.optimization_barrier((mine, *pieces))
        theirs = swap(mine)
    with jax.named_scope("probs"):
        qs, ks, dense_p, pair_p, extra_p, stats = call(
            probs_kernel, 2, 7, (blocks, sides, tall, tall, tiles, shape((24, WIDE), F32)),
            [
                pltpu.VMEM((NZ * BLOCK, WIDE), F32),
                pltpu.VMEM((NZ * BLOCK, WIDE), F32),
                pltpu.VMEM((NZ, BLOCK, WIDE), F32),
                pltpu.VMEM((8, WIDE), F32),
            ],
        )(*scalars, queries, *pieces, mine, theirs)
        all_stats = [stats, *shifts(stats, "y", NY)]
    with jax.named_scope("scores"):
        gs, dense_s, pair_s, extra_s, query_acc = call(
            scores_kernel, 2, 12, (blocks, tall, tall, tiles, shape((8, DH, WIDE), F32)),
            [
                pltpu.VMEM((2, NZ, BLOCK, DH), BF16),
                pltpu.VMEM((2, DH, NZ * BLOCK), BF16),
                pltpu.VMEM((8, 8, WIDE), F32),
            ],
            flops=4_000_000_000,
        )(
            *scalars, ks, output_grad, *pieces, own_delta, mine, theirs, dense_p, pair_p,
            extra_p,
        )
    with jax.named_scope("grads"):
        piece = shape((ROWS, WIDE), BF16)
        own_query, query1, query2, query3, keep, send = call(
            grad_kernel, 2, 13,
            (
                shape((ROWS, WIDE), F32), piece, piece, piece,
                shape((NZ, ROWS, DH), F32), shape((NZ, ROWS, DH), BF16),
            ),
            [
                pltpu.VMEM((8, WIDE, DH), BF16),
                pltpu.VMEM((8, WIDE, DH), BF16),
                pltpu.VMEM((8, WIDE), F32),
                pltpu.VMEM((2, NZ, BLOCK, DH), F32),
                pltpu.VMEM((2, NZ, BLOCK, DH), F32),
            ],
        )(
            *scalars, qs, gs, dense_p, pair_p, extra_p, dense_s, pair_s, extra_s, query_acc,
            *all_stats,
        )
    with jax.named_scope("query_sum"):
        back = [
            lax.ppermute(part, "y", [(i, (i - k) % NY) for i in range(NY)])
            for k, part in ((1, query1), (2, query2), (3, query3))
        ]
        query_grad = own_query
        for part in back:
            query_grad = query_grad + part.astype(F32)
        query_grad = query_grad.astype(BF16)
    with jax.named_scope("key_sum"):
        pair = (keep + swap(send).astype(F32)).astype(BF16)
        terms = lax.all_to_all(pair, "z", 0, 0, tiled=True)
        own_sum = jnp.sum(terms.astype(F32), axis=0).astype(BF16)
        own_sum, query_grad = lax.optimization_barrier((own_sum, query_grad))
    with jax.named_scope("heads"):
        heads = shifts(own_sum, "x", NX)
        theirs_sum = swap(jnp.stack([own_sum, *heads]))
        full = shape((ROWS, KVH * DH), BF16)
        key_grad, value_grad = call(join_kernel, 0, 5, (full, full))(
            own_sum, *heads, theirs_sum
        )
    return (query_grad, key_grad, value_grad)


def solution(mesh):
    grid = Mesh(mesh.devices.reshape(NY, NZ, NX, NCORE), ("y", "z", "x", "core"))
    rows, heads = ("y", "z"), ("x", "core")
    placed = (
        P(rows, heads),
        P(rows, None),
        P(rows, None),
        P(rows, heads),
        P(rows, heads),
        P(),
        P(),
    )
    return jax.shard_map(
        shards,
        mesh=grid,
        in_specs=placed,
        out_specs=(P(rows, heads), P(rows, None), P(rows, None)),
        check_vma=False,
    )
```

```python
import functools

import jax
import jax.numpy as jnp
from jax import lax
from jax.experimental import pallas as pl
from jax.experimental.pallas import tpu as pltpu
from jax.sharding import Mesh, PartitionSpec as P

DH = 128
QH = 16
KVH = 4
BLOCK = 128
NY, NZ, NX, NCORE = 4, 8, 4, 2
ROWS = 2 * BLOCK
WIDE = 2 * BLOCK
PACKED = ROWS + 16
SCALE = DH ** (-0.5)
EXP2_SCALE = SCALE * 1.4426950408889634
LOWEST = -1e30
VMEM_BYTES = 32 * 1024 * 1024
WHOLE_VMEM = 60 * 1024 * 1024
STEPS = ((0, 7), (1, 3), (2, 4), (6, 5))
F32 = jnp.float32
BF16 = jnp.bfloat16


def dot_nt(left, right):
    return lax.dot_general(left, right, (((1,), (1,)), ((), ())), preferred_element_type=F32)


def dot_nn(left, right):
    return lax.dot_general(left, right, (((1,), (0,)), ((), ())), preferred_element_type=F32)


def load_keys(core, z_rank, mine_ref, theirs_ref, which, target):
    for owner in range(2):

        @pl.when(core == owner)
        def _(owner=owner):
            for j in range(NZ):
                src = lax.rem(z_rank + j, NZ)
                target[owner, j] = mine_ref[src, which]
                target[1 - owner, j] = theirs_ref[src, which]


def load_queries(core, piece_refs, first_col, target, delta=None):
    def load(k, ref, first_col):
        for slot in range(2):
            for head in range(2):
                target[2 * k + slot, head * BLOCK : (head + 1) * BLOCK, :] = ref[
                    slot * BLOCK : (slot + 1) * BLOCK,
                    first_col + head * DH : first_col + (head + 1) * DH,
                ]
        if delta is not None and k:
            lines = ref[ROWS:PACKED, :WIDE].astype(F32)
            for slot in range(2):
                line = sum(lines[3 * slot + i : 3 * slot + i + 1, :] for i in range(3))
                delta[2 * k + slot] = jnp.broadcast_to(line, (8, WIDE))

    load(0, piece_refs[0], 0)
    load(1, piece_refs[1], first_col)
    load(3, piece_refs[3], first_col)
    for owner, ref in ((0, piece_refs[2]), (1, piece_refs[4])):

        @pl.when(core == owner)
        def _(ref=ref):
            load(2, ref, first_col)


def visible_tile(query_place, key_place, prompt_end):
    key_pos = key_place * BLOCK + lax.broadcasted_iota(jnp.int32, (BLOCK, WIDE), 0)
    query_pos = query_place * BLOCK + lax.rem(
        lax.broadcasted_iota(jnp.int32, (BLOCK, WIDE), 1), BLOCK
    )
    return (key_pos <= query_pos) | (key_pos < prompt_end)


def tile_max(scores):
    return jnp.max(scores.reshape(scores.shape[0] // 8, 8, WIDE), axis=0)


def tile_sum(probs):
    return jnp.sum(probs.reshape(probs.shape[0] // 8, 8, WIDE), axis=0)


def all_places(place_ref, y_rank, z_rank):
    low_places = [
        place_ref[0, lax.rem(y_rank + NY - k, NY) * NZ + z_rank] for k in range(NY)
    ]
    key_places = [place_ref[0, y_rank * NZ + lax.rem(z_rank + j, NZ)] for j in range(NZ)]
    return low_places, key_places


def ahead_of(low_places, key_places, prompt_end, k, j):
    return (key_places[j] > low_places[k]) & (key_places[j] * BLOCK < prompt_end)


def tiles_ahead(low_places, key_places, prompt_end, visit):
    flags = [
        [ahead_of(low_places, key_places, prompt_end, k, j) for j in range(NZ)] for k in range(NY)
    ]
    some = [functools.reduce(jnp.logical_or, flags[k]) for k in range(NY)]

    @pl.when(functools.reduce(jnp.logical_or, some))
    def _():
        for k in range(NY):

            @pl.when(some[k])
            def _(k=k):
                for j in range(NZ):

                    @pl.when(flags[k][j])
                    def _(j=j):
                        visit(k, j)


def probs_kernel(
    place_ref, prompt_ref, q0, q1, q2, q3, q4, mine_ref, theirs_ref,
    qs, ks, dense_ref, pair_ref, extra_ref, stats_ref, dense, pair, extra, low_peak, low_tops,
):
    y_rank, z_rank, core = (lax.axis_index(axis) for axis in ("y", "z", "core"))
    prompt_end = prompt_ref[0]
    load_keys(core, z_rank, mine_ref, theirs_ref, 0, ks)
    load_queries(core, (q0, q1, q2, q3, q4), 0, qs)
    low_places, key_places = all_places(place_ref, y_rank, z_rank)
    own_high = place_ref[1, y_rank * NZ + z_rank]
    stats_ref[...] = jnp.zeros((24, WIDE), F32)
    for k in range(NY):
        low_peak[k] = jnp.full((8, WIDE), LOWEST, F32)

    def score_ahead(k, j):
        scores = dot_nt(ks[0, j], qs[2 * k]) * EXP2_SCALE
        visible = visible_tile(low_places[k], key_places[j], prompt_end)
        scores = jnp.where(visible, scores, LOWEST)
        extra[k, j] = scores
        low_peak[k] = jnp.maximum(low_peak[k], tile_max(scores))

    tiles_ahead(low_places, key_places, prompt_end, score_ahead)
    tops = []
    for k in range(NY):
        query_high = qs[2 * k + 1]
        high = []
        low = [low_peak[k]]
        for chunk in range(NZ // 2):
            keys = ks[0, 2 * chunk : 2 * chunk + 2].reshape(2 * BLOCK, DH)
            scores = dot_nt(keys, query_high) * EXP2_SCALE
            dense[k, 2 * chunk * BLOCK : 2 * (chunk + 1) * BLOCK, :] = scores
            high.append(tile_max(scores))
        for j in range(NZ):
            is_low = key_places[j] < low_places[k]
            slot = jnp.where(is_low, 0, 1)
            scores = dot_nt(ks[slot, j], qs[2 * k + slot]) * EXP2_SCALE
            if (k, j) == (0, 0):
                scores = jnp.where(visible_tile(own_high, own_high, prompt_end), scores, LOWEST)
            pair[k, j * BLOCK : (j + 1) * BLOCK, :] = scores
            peak = tile_max(scores)
            high.append(jnp.where(is_low, LOWEST, peak))
            low.append(jnp.where(is_low, peak, LOWEST))
        if k == 0:
            scores = dot_nt(ks[0, 0], qs[0]) * EXP2_SCALE
            visible = visible_tile(low_places[0], key_places[0], prompt_end)
            scores = jnp.where(visible, scores, LOWEST)
            extra[0, 0] = scores
            low.append(tile_max(scores))
        high_top = jnp.max(functools.reduce(jnp.maximum, high), axis=0, keepdims=True)
        low_top = jnp.max(functools.reduce(jnp.maximum, low), axis=0, keepdims=True)
        tops.append((low_top, high_top))
        high_sum = jnp.zeros((8, WIDE), F32)
        low_sum = jnp.zeros((8, WIDE), F32)
        for chunk in range(NZ // 2):
            rows = slice(2 * chunk * BLOCK, 2 * (chunk + 1) * BLOCK)
            probs = jnp.exp2(dense[k, rows, :] - high_top)
            dense_ref[k, rows, :] = probs.astype(BF16)
            high_sum = high_sum + tile_sum(probs)
        for j in range(NZ):
            rows = slice(j * BLOCK, (j + 1) * BLOCK)
            is_low = key_places[j] < low_places[k]
            probs = jnp.exp2(pair[k, rows, :] - jnp.where(is_low, low_top, high_top))
            pair_ref[k, rows, :] = probs.astype(BF16)
            part = tile_sum(probs)
            high_sum = high_sum + jnp.where(is_low, 0.0, part)
            low_sum = low_sum + jnp.where(is_low, part, 0.0)
        if k == 0:
            probs = jnp.exp2(extra[0, 0] - low_top)
            extra_ref[0, 0] = probs.astype(BF16)
            low_sum = low_sum + tile_sum(probs)
        low_peak[k] = low_sum
        low_tops[k] = jnp.broadcast_to(low_top, (8, WIDE))
        row = lax.rem(y_rank + NY - k, NY) * 2
        stats_ref[pl.ds(row, 1), :] = low_top
        stats_ref[pl.ds(row + 1, 1), :] = high_top
        stats_ref[pl.ds(row + 9, 1), :] = jnp.sum(high_sum, axis=0, keepdims=True)

    def probs_ahead(k, j):
        probs = jnp.exp2((extra[k, j].reshape(BLOCK // 8, 8, WIDE) - low_tops[k][None]))
        probs = probs.reshape(BLOCK, WIDE)
        extra_ref[k, j] = probs.astype(BF16)
        low_peak[k] += tile_sum(probs)

    tiles_ahead(low_places, key_places, prompt_end, probs_ahead)
    for k in range(NY):
        row = lax.rem(y_rank + NY - k, NY) * 2
        stats_ref[pl.ds(row + 8, 1), :] = jnp.sum(low_peak[k], axis=0, keepdims=True)


def scores_kernel(
    place_ref, prompt_ref, ks, g0, g1, g2, g3, g4, own_delta, mine_ref, theirs_ref,
    dense_ref, pair_ref, extra_ref,
    gs, dense_out, pair_out, extra_out, query_acc, vs, kt, delta, low_part, chosen,
):
    y_rank, z_rank, core = (lax.axis_index(axis) for axis in ("y", "z", "core"))
    prompt_end = prompt_ref[0]
    load_keys(core, z_rank, mine_ref, theirs_ref, 1, vs)
    load_queries(core, (g0, g1, g2, g3, g4), WIDE, gs, delta)
    for slot in range(2):
        delta[slot] = jnp.broadcast_to(own_delta[slot : slot + 1, :], (8, WIDE))
    low_places, key_places = all_places(place_ref, y_rank, z_rank)
    for slot in range(2):
        for j in range(NZ):
            kt[slot, :, j * BLOCK : (j + 1) * BLOCK] = ks[slot, j].T

    def scores(probs, values, query_index):
        length = values.shape[0]
        shape = (length // 8, 8, WIDE)
        dprobs = dot_nt(values, gs[query_index]).reshape(shape) - delta[query_index][None]
        return (probs.astype(F32) * dprobs.reshape(length, WIDE)).astype(BF16)

    for k in range(NY):
        for chunk in range(NZ // 2):
            rows = slice(2 * chunk * BLOCK, 2 * (chunk + 1) * BLOCK)
            values = vs[0, 2 * chunk : 2 * chunk + 2].reshape(2 * BLOCK, DH)
            dense_out[k, rows, :] = scores(dense_ref[k, rows, :], values, 2 * k + 1)
        for j in range(NZ):
            rows = slice(j * BLOCK, (j + 1) * BLOCK)
            is_low = key_places[j] < low_places[k]
            slot = jnp.where(is_low, 0, 1)
            dscores = scores(pair_ref[k, rows, :], vs[slot, j], 2 * k + slot)
            pair_out[k, rows, :] = dscores
            low_part[rows, :] = jnp.where(is_low, dscores, jnp.zeros_like(dscores))
            chosen[:, rows] = kt[slot, :, rows]
        low_query = dot_nn(chosen[...], low_part[...])
        query_acc[2 * k] = low_query
        query_acc[2 * k + 1] = (
            dot_nn(kt[0], dense_out[k]) + dot_nn(chosen[...], pair_out[k]) - low_query
        )

    def scores_ahead(k, j):
        dscores = scores(extra_ref[k, j], vs[0, j], 2 * k)
        extra_out[k, j] = dscores
        query_acc[2 * k] += dot_nn(kt[0, :, j * BLOCK : (j + 1) * BLOCK], dscores)

    scores_ahead(0, 0)
    tiles_ahead(low_places, key_places, prompt_end, scores_ahead)


def grad_kernel(
    place_ref, prompt_ref, qs, gs, dense_p, pair_p, extra_p, dense_s, pair_s, extra_s,
    query_acc, st0, st1, st2, st3,
    own_query, query1, query2, query3, keep_ref, send_ref,
    qr, gr, factor_rows, key_acc, value_acc,
):
    y_rank, z_rank, core = (lax.axis_index(axis) for axis in ("y", "z", "core"))
    prompt_end = prompt_ref[0]
    low_places, key_places = all_places(place_ref, y_rank, z_rank)
    parts = [(ref[0:8, :], ref[8:16, :]) for ref in (st0, st1, st2, st3)]
    top = functools.reduce(jnp.maximum, [peak for peak, _ in parts])
    total = sum(part * jnp.exp2(peak - top) for peak, part in parts)
    factor_rows[...] = jnp.exp2(parts[0][0] - top) / total
    for k in range(NY):
        for slot in range(2):
            row = lax.rem(y_rank + NY - k, NY) * 2 + slot
            line = factor_rows[pl.ds(row, 1), :]
            column = jnp.broadcast_to(line, (BLOCK, WIDE)).T
            index = 2 * k + slot
            qr[index] = (qs[index].astype(F32) * column).astype(BF16)
            gr[index] = (gs[index].astype(F32) * column).astype(BF16)
            out = (own_query, query1, query2, query3)[k]
            for head in range(2):
                lanes = slice(head * BLOCK, (head + 1) * BLOCK)
                block = (query_acc[index, :, lanes] * (line[:, lanes] * SCALE)).T
                out[
                    slot * BLOCK : (slot + 1) * BLOCK, head * DH : (head + 1) * DH
                ] = block.astype(out.dtype)
    for chunk in range(NZ // 2):
        blocks = slice(2 * chunk, 2 * chunk + 2)
        rows = slice(2 * chunk * BLOCK, 2 * (chunk + 1) * BLOCK)
        key_sum = value_sum = None
        for k in range(NY):
            value_part = dot_nn(dense_p[k, rows, :], gr[2 * k + 1])
            key_part = dot_nn(dense_s[k, rows, :], qr[2 * k + 1])
            value_sum = value_part if k == 0 else value_sum + value_part
            key_sum = key_part if k == 0 else key_sum + key_part
        key_acc[0, blocks] = key_sum.reshape(2, BLOCK, DH)
        value_acc[0, blocks] = value_sum.reshape(2, BLOCK, DH)
    key_acc[1] = jnp.zeros((NZ, BLOCK, DH), F32)
    value_acc[1] = jnp.zeros((NZ, BLOCK, DH), F32)
    for j in range(NZ):
        rows = slice(j * BLOCK, (j + 1) * BLOCK)
        for k in range(NY):
            slot = jnp.where(key_places[j] < low_places[k], 0, 1)
            value_acc[slot, j] += dot_nn(pair_p[k, rows, :], gr[2 * k + slot])
            key_acc[slot, j] += dot_nn(pair_s[k, rows, :], qr[2 * k + slot])

    def grads_ahead(k, j):
        value_acc[0, j] += dot_nn(extra_p[k, j], gr[2 * k])
        key_acc[0, j] += dot_nn(extra_s[k, j], qr[2 * k])

    grads_ahead(0, 0)
    tiles_ahead(low_places, key_places, prompt_end, grads_ahead)

    for owner in range(2):

        @pl.when(core == owner)
        def _(owner=owner):
            for t, steps in enumerate(STEPS):
                for j, ref in ((steps[owner], keep_ref), (steps[1 - owner], send_ref)):
                    for slot in range(2):
                        rows = slice(slot * BLOCK, (slot + 1) * BLOCK)
                        ref[t, rows, :DH] = (key_acc[slot, j] * SCALE).astype(ref.dtype)
                        ref[t, rows, DH:] = value_acc[slot, j].astype(ref.dtype)


def prepare_kernel(
    queries_ref, saved_ref, grad_ref, key_ref, value_ref, out_ref, spread_ref, delta_ref,
    saved, sems,
):
    first_row = pl.multiple_of(lax.axis_index("core") * BLOCK, BLOCK)
    first_col = pl.multiple_of(lax.axis_index("x") * DH, DH)
    own = (pl.ds(first_row, BLOCK), pl.ds(first_col, DH))
    copies = [
        pltpu.make_async_copy(source, target, sems.at[i])
        for i, (source, target) in enumerate(
            (
                (key_ref.at[own], spread_ref.at[0, 0]),
                (value_ref.at[own], spread_ref.at[0, 1]),
                (grad_ref, out_ref.at[pl.ds(0, ROWS), pl.ds(WIDE, WIDE)]),
                (saved_ref, saved),
                (queries_ref, out_ref.at[pl.ds(0, ROWS), pl.ds(0, WIDE)]),
            )
        )
    ]
    for copy in copies:
        copy.start()
    copies[0].wait()
    copies[1].wait()
    for z in range(1, NZ):
        spread_ref[z] = spread_ref[0]
    copies[2].wait()
    copies[3].wait()
    lines = []
    for slot in range(2):
        rows = slice(slot * BLOCK, (slot + 1) * BLOCK)
        heads = []
        for head in range(2):
            columns = slice(head * DH, (head + 1) * DH)
            beside = slice(WIDE + head * DH, WIDE + (head + 1) * DH)
            product = out_ref[rows, beside].astype(F32) * saved[rows, columns].astype(F32)
            heads.append(jnp.sum(product.T, axis=0, keepdims=True))
        rest = jnp.concatenate(heads, axis=1)
        for _ in range(3):
            term = rest.astype(BF16).astype(F32)
            lines.append(term)
            rest = rest - term
        delta_ref[slot : slot + 1, :] = jnp.concatenate(heads, axis=1)
    lines.append(jnp.zeros((PACKED - ROWS - len(lines), WIDE), F32))
    out_ref[ROWS:, :WIDE] = jnp.concatenate(lines, axis=0).astype(BF16)
    out_ref[ROWS:, WIDE:] = jnp.zeros((PACKED - ROWS, WIDE), BF16)
    copies[4].wait()


def join_kernel(own_ref, p1, p2, p3, theirs_ref, key_ref, value_ref):
    x_rank, core = lax.axis_index("x"), lax.axis_index("core")
    for k, ref in enumerate((own_ref, p1, p2, p3)):
        column = pl.multiple_of(lax.rem(x_rank + NX - k, NX) * DH, DH)
        for owner in range(2):

            @pl.when(core == owner)
            def _(owner=owner, ref=ref, k=k, column=column):
                outs = (key_ref, value_ref)
                outs[owner][:, pl.ds(column, DH)] = ref[...]
                outs[1 - owner][:, pl.ds(column, DH)] = theirs_ref[k]


def call(kernel, n_scalars, n_arrays, out_shape, scratch=(), flops=0, far_in=0):
    return pl.pallas_call(
        kernel,
        out_shape=out_shape,
        in_specs=[pl.BlockSpec(memory_space=pltpu.SMEM)] * n_scalars
        + [pl.BlockSpec(memory_space=pl.ANY)] * far_in
        + [pl.BlockSpec(memory_space=pltpu.VMEM)] * n_arrays,
        out_specs=jax.tree.map(lambda _: pl.BlockSpec(memory_space=pltpu.VMEM), out_shape),
        scratch_shapes=list(scratch),
        compiler_params=pltpu.CompilerParams(vmem_limit_bytes=WHOLE_VMEM if far_in else VMEM_BYTES),
        cost_estimate=pl.CostEstimate(flops=flops, bytes_accessed=0, transcendentals=0),
    )


def shifts(array, axis, size):
    return [
        lax.ppermute(array, axis, [(i, (i + k) % size) for i in range(size)])
        for k in range(1, size)
    ]


def step_of_one_core(mover, step):
    return [
        (y * NCORE + core, (y + step) % NY * NCORE + core if core == mover else y * NCORE + core)
        for y in range(NY)
        for core in range(NCORE)
    ]


def key_pairs(steps):
    return [
        (z * NCORE + core, (z + steps[core]) % NZ * NCORE + core)
        for z in range(NZ)
        for core in range(NCORE)
    ]


def shards(
    queries, key_states, value_states, saved_output, output_grad, block_place, prompt_length
):
    scalars = (block_place.T, prompt_length)
    shape = jax.ShapeDtypeStruct

    def swap(array):
        return lax.ppermute(array, "core", [(0, 1), (1, 0)])

    blocks = shape((8, WIDE, DH), BF16)
    sides = shape((2, NZ, BLOCK, DH), BF16)
    tall = shape((NY, NZ * BLOCK, WIDE), BF16)
    tiles = shape((NY, NZ, BLOCK, WIDE), BF16)
    with jax.named_scope("gather"):
        packed, spread, own_delta = call(
            prepare_kernel, 0, 0,
            (
                shape((PACKED, 2 * WIDE), BF16), shape((NZ, 2, BLOCK, DH), BF16),
                shape((8, WIDE), F32),
            ),
            [pltpu.VMEM((ROWS, WIDE), BF16), pltpu.SemaphoreType.DMA((5,))],
            far_in=5,
        )(queries, saved_output, output_grad, key_states, value_states)
        down = lax.ppermute(packed, "y", [(i, (i - 1) % NY) for i in range(NY)])
        up = lax.ppermute(packed, "y", [(i, (i + 1) % NY) for i in range(NY)])
        far = lax.ppermute(packed, ("y", "core"), step_of_one_core(0, 2))
        relayed = lax.ppermute(down, ("y", "core"), step_of_one_core(1, -1))
        pieces = [up, far, down, relayed]
        mine = lax.all_to_all(spread, "z", 0, 0, tiled=True)
        own_query = packed[:ROWS, :WIDE]
        mine, own_query, *pieces = lax.optimization_barrier((mine, own_query, *pieces))
        theirs = swap(mine)
    with jax.named_scope("probs"):
        qs, ks, dense_p, pair_p, extra_p, stats = call(
            probs_kernel, 2, 7, (blocks, sides, tall, tall, tiles, shape((24, WIDE), F32)),
            [
                pltpu.VMEM((NY, NZ * BLOCK, WIDE), F32),
                pltpu.VMEM((NY, NZ * BLOCK, WIDE), F32),
                pltpu.VMEM((NY, NZ, BLOCK, WIDE), F32),
                pltpu.VMEM((NY, 8, WIDE), F32),
                pltpu.VMEM((NY, 8, WIDE), F32),
            ],
        )(*scalars, own_query, *pieces, mine, theirs)
        all_stats = [stats, *shifts(stats, "y", NY)]
    with jax.named_scope("scores"):
        gs, dense_s, pair_s, extra_s, query_acc = call(
            scores_kernel, 2, 12, (blocks, tall, tall, tiles, shape((8, DH, WIDE), F32)),
            [
                pltpu.VMEM((2, NZ, BLOCK, DH), BF16),
                pltpu.VMEM((2, DH, NZ * BLOCK), BF16),
                pltpu.VMEM((8, 8, WIDE), F32),
                pltpu.VMEM((NZ * BLOCK, WIDE), BF16),
                pltpu.VMEM((DH, NZ * BLOCK), BF16),
            ],
            flops=4_000_000_000,
        )(
            *scalars, ks, output_grad, *pieces, own_delta, mine, theirs, dense_p, pair_p,
            extra_p,
        )
    with jax.named_scope("grads"):
        piece = shape((ROWS, WIDE), BF16)
        own_query, query1, query2, query3, keep, send = call(
            grad_kernel, 2, 13,
            (
                shape((ROWS, WIDE), F32), piece, piece, piece,
                shape((len(STEPS), ROWS, 2 * DH), F32),
                shape((len(STEPS), ROWS, 2 * DH), BF16),
            ),
            [
                pltpu.VMEM((8, WIDE, DH), BF16),
                pltpu.VMEM((8, WIDE, DH), BF16),
                pltpu.VMEM((8, WIDE), F32),
                pltpu.VMEM((2, NZ, BLOCK, DH), F32),
                pltpu.VMEM((2, NZ, BLOCK, DH), F32),
            ],
        )(
            *scalars, qs, gs, dense_p, pair_p, extra_p, dense_s, pair_s, extra_s, query_acc,
            *all_stats,
        )
    with jax.named_scope("key_sum"):
        received = swap(send)
        parts = {}
        for t in (2, 3, 1, 0):
            pair = (keep[t] + received[t].astype(F32)).astype(BF16)
            parts[t] = lax.ppermute(pair, ("z", "core"), key_pairs(STEPS[t]))
        back = [
            lax.ppermute(part, "y", [(i, (i - k) % NY) for i in range(NY)])
            for k, part in ((1, query1), (2, query2), (3, query3))
        ]
        parts, back = lax.optimization_barrier((parts, back))
        total = sum(parts[t].astype(F32) for t in range(len(STEPS)))
        core = lax.axis_index("core")
        kept = jnp.where(core == 0, total[:, :DH], total[:, DH:])
        sent = jnp.where(core == 0, total[:, DH:], total[:, :DH]).astype(BF16)
        own_sum = (kept + swap(sent).astype(F32)).astype(BF16)
    with jax.named_scope("heads"):
        heads = shifts(own_sum, "x", NX)
        theirs_sum = swap(jnp.stack([own_sum, *heads]))
        full = shape((ROWS, KVH * DH), BF16)
        key_grad, value_grad = call(join_kernel, 0, 5, (full, full))(
            own_sum, *heads, theirs_sum
        )
    with jax.named_scope("query_sum"):
        query_grad = own_query
        for part in back:
            query_grad = query_grad + part.astype(F32)
        query_grad = query_grad.astype(BF16)
    return (query_grad, key_grad, value_grad)


def solution(mesh):
    grid = Mesh(mesh.devices.reshape(NY, NZ, NX, NCORE), ("y", "z", "x", "core"))
    rows, heads = ("y", "z"), ("x", "core")
    placed = (
        P(rows, heads),
        P(rows, None),
        P(rows, None),
        P(rows, heads),
        P(rows, heads),
        P(),
        P(),
    )
    return jax.shard_map(
        shards,
        mesh=grid,
        in_specs=placed,
        out_specs=(P(rows, heads), P(rows, None), P(rows, None)),
        check_vma=False,
    )
```

```python
import functools

import jax
import jax.numpy as jnp
from jax import lax
from jax.experimental import pallas as pl
from jax.experimental.pallas import tpu as pltpu
from jax.sharding import Mesh, PartitionSpec as P

DH = 128
QH = 16
KVH = 4
BLOCK = 128
NY, NZ, NX, NCORE = 4, 8, 4, 2
ROWS = 2 * BLOCK
WIDE = 2 * BLOCK
PACKED = ROWS + 16
SCALE = DH ** (-0.5)
EXP2_SCALE = SCALE * 1.4426950408889634
LOWEST = -1e30
VMEM_BYTES = 32 * 1024 * 1024
WHOLE_VMEM = 60 * 1024 * 1024
STEPS = ((0, 1), (2, 6), (3, 5), (7, 4))
F32 = jnp.float32
BF16 = jnp.bfloat16


def dot_nt(left, right):
    return lax.dot_general(left, right, (((1,), (1,)), ((), ())), preferred_element_type=F32)


def dot_nn(left, right):
    return lax.dot_general(left, right, (((1,), (0,)), ((), ())), preferred_element_type=F32)


def load_keys(core, z_rank, mine_ref, theirs_ref, which, target):
    for owner in range(2):

        @pl.when(core == owner)
        def _(owner=owner):
            for j in range(NZ):
                src = lax.rem(z_rank + j, NZ)
                target[owner, j] = mine_ref[src, which]
                target[1 - owner, j] = theirs_ref[src, which]


def load_queries(core, piece_refs, first_col, target, delta=None):
    def load(k, ref, first_col):
        for slot in range(2):
            for head in range(2):
                target[2 * k + slot, head * BLOCK : (head + 1) * BLOCK, :] = ref[
                    slot * BLOCK : (slot + 1) * BLOCK,
                    first_col + head * DH : first_col + (head + 1) * DH,
                ]
        if delta is not None and k:
            lines = ref[ROWS:PACKED, :WIDE].astype(F32)
            for slot in range(2):
                line = sum(lines[3 * slot + i : 3 * slot + i + 1, :] for i in range(3))
                delta[2 * k + slot] = jnp.broadcast_to(line, (8, WIDE))

    load(0, piece_refs[0], 0)
    load(1, piece_refs[1], first_col)
    load(3, piece_refs[3], first_col)
    for owner, ref in ((0, piece_refs[2]), (1, piece_refs[4])):

        @pl.when(core == owner)
        def _(ref=ref):
            load(2, ref, first_col)


def visible_tile(query_place, key_place, prompt_end):
    key_pos = key_place * BLOCK + lax.broadcasted_iota(jnp.int32, (BLOCK, WIDE), 0)
    query_pos = query_place * BLOCK + lax.rem(
        lax.broadcasted_iota(jnp.int32, (BLOCK, WIDE), 1), BLOCK
    )
    return (key_pos <= query_pos) | (key_pos < prompt_end)


def tile_max(scores):
    return jnp.max(scores.reshape(scores.shape[0] // 8, 8, WIDE), axis=0)


def tile_sum(probs):
    return jnp.sum(probs.reshape(probs.shape[0] // 8, 8, WIDE), axis=0)


def all_places(place_ref, y_rank, z_rank):
    low_places = [
        place_ref[0, lax.rem(y_rank + NY - k, NY) * NZ + z_rank] for k in range(NY)
    ]
    key_places = [place_ref[0, y_rank * NZ + lax.rem(z_rank + j, NZ)] for j in range(NZ)]
    return low_places, key_places


def ahead_of(low_places, key_places, prompt_end, k, j):
    return (key_places[j] > low_places[k]) & (key_places[j] * BLOCK < prompt_end)


def tiles_ahead(low_places, key_places, prompt_end, visit):
    flags = [
        [ahead_of(low_places, key_places, prompt_end, k, j) for j in range(NZ)] for k in range(NY)
    ]
    some = [functools.reduce(jnp.logical_or, flags[k]) for k in range(NY)]

    @pl.when(functools.reduce(jnp.logical_or, some))
    def _():
        for k in range(NY):

            @pl.when(some[k])
            def _(k=k):
                for j in range(NZ):

                    @pl.when(flags[k][j])
                    def _(j=j):
                        visit(k, j)


def probs_kernel(
    place_ref, prompt_ref, q0, q1, q2, q3, q4, mine_ref, theirs_ref,
    qs, ks, dense_ref, pair_ref, extra_ref, stats_ref, dense, pair, extra, low_peak, low_tops,
):
    y_rank, z_rank, core = (lax.axis_index(axis) for axis in ("y", "z", "core"))
    prompt_end = prompt_ref[0]
    load_keys(core, z_rank, mine_ref, theirs_ref, 0, ks)
    load_queries(core, (q0, q1, q2, q3, q4), 0, qs)
    low_places, key_places = all_places(place_ref, y_rank, z_rank)
    own_high = place_ref[1, y_rank * NZ + z_rank]
    stats_ref[...] = jnp.zeros((24, WIDE), F32)
    for k in range(NY):
        low_peak[k] = jnp.full((8, WIDE), LOWEST, F32)

    def score_ahead(k, j):
        scores = dot_nt(ks[0, j], qs[2 * k]) * EXP2_SCALE
        visible = visible_tile(low_places[k], key_places[j], prompt_end)
        scores = jnp.where(visible, scores, LOWEST)
        extra[k, j] = scores
        low_peak[k] = jnp.maximum(low_peak[k], tile_max(scores))

    tiles_ahead(low_places, key_places, prompt_end, score_ahead)
    tops = []
    for k in range(NY):
        query_high = qs[2 * k + 1]
        high = []
        low = [low_peak[k]]
        for chunk in range(NZ // 2):
            keys = ks[0, 2 * chunk : 2 * chunk + 2].reshape(2 * BLOCK, DH)
            scores = dot_nt(keys, query_high) * EXP2_SCALE
            dense[k, 2 * chunk * BLOCK : 2 * (chunk + 1) * BLOCK, :] = scores
            high.append(tile_max(scores))
        for j in range(NZ):
            is_low = key_places[j] < low_places[k]
            slot = jnp.where(is_low, 0, 1)
            scores = dot_nt(ks[slot, j], qs[2 * k + slot]) * EXP2_SCALE
            if (k, j) == (0, 0):
                scores = jnp.where(visible_tile(own_high, own_high, prompt_end), scores, LOWEST)
            pair[k, j * BLOCK : (j + 1) * BLOCK, :] = scores
            peak = tile_max(scores)
            high.append(jnp.where(is_low, LOWEST, peak))
            low.append(jnp.where(is_low, peak, LOWEST))
        if k == 0:
            scores = dot_nt(ks[0, 0], qs[0]) * EXP2_SCALE
            visible = visible_tile(low_places[0], key_places[0], prompt_end)
            scores = jnp.where(visible, scores, LOWEST)
            extra[0, 0] = scores
            low.append(tile_max(scores))
        high_top = jnp.max(functools.reduce(jnp.maximum, high), axis=0, keepdims=True)
        low_top = jnp.max(functools.reduce(jnp.maximum, low), axis=0, keepdims=True)
        tops.append((low_top, high_top))
        high_sum = jnp.zeros((8, WIDE), F32)
        low_sum = jnp.zeros((8, WIDE), F32)
        for chunk in range(NZ // 2):
            rows = slice(2 * chunk * BLOCK, 2 * (chunk + 1) * BLOCK)
            probs = jnp.exp2(dense[k, rows, :] - high_top)
            dense_ref[k, rows, :] = probs.astype(BF16)
            high_sum = high_sum + tile_sum(probs)
        for j in range(NZ):
            rows = slice(j * BLOCK, (j + 1) * BLOCK)
            is_low = key_places[j] < low_places[k]
            probs = jnp.exp2(pair[k, rows, :] - jnp.where(is_low, low_top, high_top))
            pair_ref[k, rows, :] = probs.astype(BF16)
            part = tile_sum(probs)
            high_sum = high_sum + jnp.where(is_low, 0.0, part)
            low_sum = low_sum + jnp.where(is_low, part, 0.0)
        if k == 0:
            probs = jnp.exp2(extra[0, 0] - low_top)
            extra_ref[0, 0] = probs.astype(BF16)
            low_sum = low_sum + tile_sum(probs)
        low_peak[k] = low_sum
        low_tops[k] = jnp.broadcast_to(low_top, (8, WIDE))
        row = lax.rem(y_rank + NY - k, NY) * 2
        stats_ref[pl.ds(row, 1), :] = low_top
        stats_ref[pl.ds(row + 1, 1), :] = high_top
        stats_ref[pl.ds(row + 9, 1), :] = jnp.sum(high_sum, axis=0, keepdims=True)

    def probs_ahead(k, j):
        probs = jnp.exp2((extra[k, j].reshape(BLOCK // 8, 8, WIDE) - low_tops[k][None]))
        probs = probs.reshape(BLOCK, WIDE)
        extra_ref[k, j] = probs.astype(BF16)
        low_peak[k] += tile_sum(probs)

    tiles_ahead(low_places, key_places, prompt_end, probs_ahead)
    for k in range(NY):
        row = lax.rem(y_rank + NY - k, NY) * 2
        stats_ref[pl.ds(row + 8, 1), :] = jnp.sum(low_peak[k], axis=0, keepdims=True)


def scores_kernel(
    place_ref, prompt_ref, ks, g0, g1, g2, g3, g4, own_delta, mine_ref, theirs_ref,
    dense_ref, pair_ref, extra_ref,
    gs, dense_out, pair_out, extra_out, query_acc, vs, kt, delta, low_part, chosen,
):
    y_rank, z_rank, core = (lax.axis_index(axis) for axis in ("y", "z", "core"))
    prompt_end = prompt_ref[0]
    load_keys(core, z_rank, mine_ref, theirs_ref, 1, vs)
    load_queries(core, (g0, g1, g2, g3, g4), WIDE, gs, delta)
    for slot in range(2):
        delta[slot] = jnp.broadcast_to(own_delta[slot : slot + 1, :], (8, WIDE))
    low_places, key_places = all_places(place_ref, y_rank, z_rank)
    for slot in range(2):
        for j in range(NZ):
            kt[slot, :, j * BLOCK : (j + 1) * BLOCK] = ks[slot, j].T

    def scores(probs, values, query_index):
        length = values.shape[0]
        shape = (length // 8, 8, WIDE)
        dprobs = dot_nt(values, gs[query_index]).reshape(shape) - delta[query_index][None]
        return (probs.astype(F32) * dprobs.reshape(length, WIDE)).astype(BF16)

    for k in range(NY):
        for chunk in range(NZ // 2):
            rows = slice(2 * chunk * BLOCK, 2 * (chunk + 1) * BLOCK)
            values = vs[0, 2 * chunk : 2 * chunk + 2].reshape(2 * BLOCK, DH)
            dense_out[k, rows, :] = scores(dense_ref[k, rows, :], values, 2 * k + 1)
        for j in range(NZ):
            rows = slice(j * BLOCK, (j + 1) * BLOCK)
            is_low = key_places[j] < low_places[k]
            slot = jnp.where(is_low, 0, 1)
            dscores = scores(pair_ref[k, rows, :], vs[slot, j], 2 * k + slot)
            pair_out[k, rows, :] = dscores
            low_part[rows, :] = jnp.where(is_low, dscores, jnp.zeros_like(dscores))
            chosen[:, rows] = kt[slot, :, rows]
        low_query = dot_nn(chosen[...], low_part[...])
        query_acc[2 * k] = low_query
        query_acc[2 * k + 1] = (
            dot_nn(kt[0], dense_out[k]) + dot_nn(chosen[...], pair_out[k]) - low_query
        )

    def scores_ahead(k, j):
        dscores = scores(extra_ref[k, j], vs[0, j], 2 * k)
        extra_out[k, j] = dscores
        query_acc[2 * k] += dot_nn(kt[0, :, j * BLOCK : (j + 1) * BLOCK], dscores)

    scores_ahead(0, 0)
    tiles_ahead(low_places, key_places, prompt_end, scores_ahead)


def grad_kernel(
    place_ref, prompt_ref, qs, gs, dense_p, pair_p, extra_p, dense_s, pair_s, extra_s,
    query_acc, st0, st1, st2, st3,
    own_query, query1, query2, query3, keep_ref, send_ref,
    qr, gr, factor_rows, key_acc, value_acc,
):
    y_rank, z_rank, core = (lax.axis_index(axis) for axis in ("y", "z", "core"))
    prompt_end = prompt_ref[0]
    low_places, key_places = all_places(place_ref, y_rank, z_rank)
    parts = [(ref[0:8, :], ref[8:16, :]) for ref in (st0, st1, st2, st3)]
    top = functools.reduce(jnp.maximum, [peak for peak, _ in parts])
    total = sum(part * jnp.exp2(peak - top) for peak, part in parts)
    factor_rows[...] = jnp.exp2(parts[0][0] - top) / total
    for k in range(NY):
        for slot in range(2):
            row = lax.rem(y_rank + NY - k, NY) * 2 + slot
            line = factor_rows[pl.ds(row, 1), :]
            column = jnp.broadcast_to(line, (BLOCK, WIDE)).T
            index = 2 * k + slot
            qr[index] = (qs[index].astype(F32) * column).astype(BF16)
            gr[index] = (gs[index].astype(F32) * column).astype(BF16)
            out = (own_query, query1, query2, query3)[k]
            for head in range(2):
                lanes = slice(head * BLOCK, (head + 1) * BLOCK)
                block = (query_acc[index, :, lanes] * (line[:, lanes] * SCALE)).T
                out[
                    slot * BLOCK : (slot + 1) * BLOCK, head * DH : (head + 1) * DH
                ] = block.astype(out.dtype)
    for chunk in range(NZ // 2):
        blocks = slice(2 * chunk, 2 * chunk + 2)
        rows = slice(2 * chunk * BLOCK, 2 * (chunk + 1) * BLOCK)
        key_sum = value_sum = None
        for k in range(NY):
            value_part = dot_nn(dense_p[k, rows, :], gr[2 * k + 1])
            key_part = dot_nn(dense_s[k, rows, :], qr[2 * k + 1])
            value_sum = value_part if k == 0 else value_sum + value_part
            key_sum = key_part if k == 0 else key_sum + key_part
        key_acc[0, blocks] = key_sum.reshape(2, BLOCK, DH)
        value_acc[0, blocks] = value_sum.reshape(2, BLOCK, DH)
    key_acc[1] = jnp.zeros((NZ, BLOCK, DH), F32)
    value_acc[1] = jnp.zeros((NZ, BLOCK, DH), F32)
    for j in range(NZ):
        rows = slice(j * BLOCK, (j + 1) * BLOCK)
        for k in range(NY):
            slot = jnp.where(key_places[j] < low_places[k], 0, 1)
            value_acc[slot, j] += dot_nn(pair_p[k, rows, :], gr[2 * k + slot])
            key_acc[slot, j] += dot_nn(pair_s[k, rows, :], qr[2 * k + slot])

    def grads_ahead(k, j):
        value_acc[0, j] += dot_nn(extra_p[k, j], gr[2 * k])
        key_acc[0, j] += dot_nn(extra_s[k, j], qr[2 * k])

    grads_ahead(0, 0)
    tiles_ahead(low_places, key_places, prompt_end, grads_ahead)

    for owner in range(2):

        @pl.when(core == owner)
        def _(owner=owner):
            for t, steps in enumerate(STEPS):
                for j, ref in ((steps[owner], keep_ref), (steps[1 - owner], send_ref)):
                    for slot in range(2):
                        rows = slice(slot * BLOCK, (slot + 1) * BLOCK)
                        ref[t, rows, :DH] = (key_acc[slot, j] * SCALE).astype(ref.dtype)
                        ref[t, rows, DH:] = value_acc[slot, j].astype(ref.dtype)


def prepare_kernel(
    queries_ref, saved_ref, grad_ref, key_ref, value_ref, out_ref, spread_ref, delta_ref,
    saved, sems,
):
    first_row = pl.multiple_of(lax.axis_index("core") * BLOCK, BLOCK)
    first_col = pl.multiple_of(lax.axis_index("x") * DH, DH)
    own = (pl.ds(first_row, BLOCK), pl.ds(first_col, DH))
    copies = [
        pltpu.make_async_copy(source, target, sems.at[i])
        for i, (source, target) in enumerate(
            (
                (key_ref.at[own], spread_ref.at[0, 0]),
                (value_ref.at[own], spread_ref.at[0, 1]),
                (grad_ref, out_ref.at[pl.ds(0, ROWS), pl.ds(WIDE, WIDE)]),
                (saved_ref, saved),
                (queries_ref, out_ref.at[pl.ds(0, ROWS), pl.ds(0, WIDE)]),
            )
        )
    ]
    for copy in copies:
        copy.start()
    copies[0].wait()
    copies[1].wait()
    for z in range(1, NZ):
        spread_ref[z] = spread_ref[0]
    copies[2].wait()
    copies[3].wait()
    lines = []
    for slot in range(2):
        rows = slice(slot * BLOCK, (slot + 1) * BLOCK)
        heads = []
        for head in range(2):
            columns = slice(head * DH, (head + 1) * DH)
            beside = slice(WIDE + head * DH, WIDE + (head + 1) * DH)
            product = out_ref[rows, beside].astype(F32) * saved[rows, columns].astype(F32)
            heads.append(jnp.sum(product.T, axis=0, keepdims=True))
        rest = jnp.concatenate(heads, axis=1)
        for _ in range(3):
            term = rest.astype(BF16).astype(F32)
            lines.append(term)
            rest = rest - term
        delta_ref[slot : slot + 1, :] = jnp.concatenate(heads, axis=1)
    lines.append(jnp.zeros((PACKED - ROWS - len(lines), WIDE), F32))
    out_ref[ROWS:, :WIDE] = jnp.concatenate(lines, axis=0).astype(BF16)
    out_ref[ROWS:, WIDE:] = jnp.zeros((PACKED - ROWS, WIDE), BF16)
    copies[4].wait()


def join_kernel(both_ref, near_ref, far_ref, theirs_ref, key_ref, value_ref):
    x_rank, core = lax.axis_index("x"), lax.axis_index("core")

    def place(out_ref, k, block):
        column = pl.multiple_of(lax.rem(x_rank + NX - k, NX) * DH, DH)
        out_ref[:, pl.ds(column, DH)] = block

    for owner in range(2):

        @pl.when(core == owner)
        def _(owner=owner):
            own_out, other_out = (key_ref, value_ref) if owner == 0 else (value_ref, key_ref)
            near, opposite = (1, 3) if owner == 0 else (3, 1)
            for k, ref in ((0, both_ref), (near, near_ref), (opposite, theirs_ref)):
                place(key_ref, k, ref[:, :DH])
                place(value_ref, k, ref[:, DH : 2 * DH])
            place(own_out, 2, far_ref[...])
            place(other_out, 2, theirs_ref[:, 2 * DH :])


def call(kernel, n_scalars, n_arrays, out_shape, scratch=(), flops=0, far_in=0):
    return pl.pallas_call(
        kernel,
        out_shape=out_shape,
        in_specs=[pl.BlockSpec(memory_space=pltpu.SMEM)] * n_scalars
        + [pl.BlockSpec(memory_space=pl.ANY)] * far_in
        + [pl.BlockSpec(memory_space=pltpu.VMEM)] * n_arrays,
        out_specs=jax.tree.map(lambda _: pl.BlockSpec(memory_space=pltpu.VMEM), out_shape),
        scratch_shapes=list(scratch),
        compiler_params=pltpu.CompilerParams(vmem_limit_bytes=WHOLE_VMEM if far_in else VMEM_BYTES),
        cost_estimate=pl.CostEstimate(flops=flops, bytes_accessed=0, transcendentals=0),
    )


def shifts(array, axis, size):
    return [
        lax.ppermute(array, axis, [(i, (i + k) % size) for i in range(size)])
        for k in range(1, size)
    ]


def step_of_one_core(mover, step):
    return [
        (y * NCORE + core, (y + step) % NY * NCORE + core if core == mover else y * NCORE + core)
        for y in range(NY)
        for core in range(NCORE)
    ]


def key_pairs(steps):
    return [
        (z * NCORE + core, (z + steps[core]) % NZ * NCORE + core)
        for z in range(NZ)
        for core in range(NCORE)
    ]


def shards(
    queries, key_states, value_states, saved_output, output_grad, block_place, prompt_length
):
    scalars = (block_place.T, prompt_length)
    shape = jax.ShapeDtypeStruct

    def swap(array):
        return lax.ppermute(array, "core", [(0, 1), (1, 0)])

    blocks = shape((8, WIDE, DH), BF16)
    sides = shape((2, NZ, BLOCK, DH), BF16)
    tall = shape((NY, NZ * BLOCK, WIDE), BF16)
    tiles = shape((NY, NZ, BLOCK, WIDE), BF16)
    with jax.named_scope("gather"):
        packed, spread, own_delta = call(
            prepare_kernel, 0, 0,
            (
                shape((PACKED, 2 * WIDE), BF16), shape((NZ, 2, BLOCK, DH), BF16),
                shape((8, WIDE), F32),
            ),
            [pltpu.VMEM((ROWS, WIDE), BF16), pltpu.SemaphoreType.DMA((5,))],
            far_in=5,
        )(queries, saved_output, output_grad, key_states, value_states)
        down = lax.ppermute(packed, "y", [(i, (i - 1) % NY) for i in range(NY)])
        up = lax.ppermute(packed, "y", [(i, (i + 1) % NY) for i in range(NY)])
        far = lax.ppermute(packed, ("y", "core"), step_of_one_core(0, 2))
        relayed = lax.ppermute(down, ("y", "core"), step_of_one_core(1, -1))
        pieces = [up, far, down, relayed]
        mine = lax.all_to_all(spread, "z", 0, 0, tiled=True)
        own_query = packed[:ROWS, :WIDE]
        mine, own_query, *pieces = lax.optimization_barrier((mine, own_query, *pieces))
        theirs = swap(mine)
    with jax.named_scope("probs"):
        qs, ks, dense_p, pair_p, extra_p, stats = call(
            probs_kernel, 2, 7, (blocks, sides, tall, tall, tiles, shape((24, WIDE), F32)),
            [
                pltpu.VMEM((NY, NZ * BLOCK, WIDE), F32),
                pltpu.VMEM((NY, NZ * BLOCK, WIDE), F32),
                pltpu.VMEM((NY, NZ, BLOCK, WIDE), F32),
                pltpu.VMEM((NY, 8, WIDE), F32),
                pltpu.VMEM((NY, 8, WIDE), F32),
            ],
        )(*scalars, own_query, *pieces, mine, theirs)
        all_stats = [stats, *shifts(stats, "y", NY)]
    with jax.named_scope("scores"):
        gs, dense_s, pair_s, extra_s, query_acc = call(
            scores_kernel, 2, 12, (blocks, tall, tall, tiles, shape((8, DH, WIDE), F32)),
            [
                pltpu.VMEM((2, NZ, BLOCK, DH), BF16),
                pltpu.VMEM((2, DH, NZ * BLOCK), BF16),
                pltpu.VMEM((8, 8, WIDE), F32),
                pltpu.VMEM((NZ * BLOCK, WIDE), BF16),
                pltpu.VMEM((DH, NZ * BLOCK), BF16),
            ],
            flops=4_000_000_000,
        )(
            *scalars, ks, output_grad, *pieces, own_delta, mine, theirs, dense_p, pair_p,
            extra_p,
        )
    with jax.named_scope("grads"):
        piece = shape((ROWS, WIDE), BF16)
        own_query, query1, query2, query3, keep, send = call(
            grad_kernel, 2, 13,
            (
                shape((ROWS, WIDE), F32), piece, piece, piece,
                shape((len(STEPS), ROWS, 2 * DH), F32),
                shape((len(STEPS), ROWS, 2 * DH), BF16),
            ),
            [
                pltpu.VMEM((8, WIDE, DH), BF16),
                pltpu.VMEM((8, WIDE, DH), BF16),
                pltpu.VMEM((8, WIDE), F32),
                pltpu.VMEM((2, NZ, BLOCK, DH), F32),
                pltpu.VMEM((2, NZ, BLOCK, DH), F32),
            ],
        )(
            *scalars, qs, gs, dense_p, pair_p, extra_p, dense_s, pair_s, extra_s, query_acc,
            *all_stats,
        )
    with jax.named_scope("key_sum"):
        received = swap(send)
        parts = {}
        for t in (2, 3, 1, 0):
            pair = (keep[t] + received[t].astype(F32)).astype(BF16)
            parts[t] = lax.ppermute(pair, ("z", "core"), key_pairs(STEPS[t]))
        back = [
            lax.ppermute(part, "y", [(i, (i - k) % NY) for i in range(NY)])
            for k, part in ((1, query1), (2, query2), (3, query3))
        ]
        parts, back = lax.optimization_barrier((parts, back))
        total = sum(parts[t].astype(F32) for t in range(len(STEPS)))
        rounded = lax.optimization_barrier(total.astype(BF16))
        both = (rounded.astype(F32) + swap(rounded).astype(F32)).astype(BF16)
    with jax.named_scope("heads"):
        own_half = lax.dynamic_slice(both, (0, lax.axis_index("core") * DH), (ROWS, DH))
        far = lax.ppermute(own_half, "x", [(i, (i + 2) % NX) for i in range(NX)])
        near = lax.ppermute(
            both, ("x", "core"),
            [
                (x * NCORE + c, (x + (1, -1)[c]) % NX * NCORE + c)
                for x in range(NX)
                for c in range(NCORE)
            ],
        )
        theirs = swap(jnp.concatenate([near, far], axis=1))
        full = shape((ROWS, KVH * DH), BF16)
        key_grad, value_grad = call(join_kernel, 0, 4, (full, full))(
            both, near, far, theirs
        )
    with jax.named_scope("query_sum"):
        query_grad = own_query
        for part in back:
            query_grad = query_grad + part.astype(F32)
        query_grad = query_grad.astype(BF16)
    return (query_grad, key_grad, value_grad)


def solution(mesh):
    grid = Mesh(mesh.devices.reshape(NY, NZ, NX, NCORE), ("y", "z", "x", "core"))
    rows, heads = ("y", "z"), ("x", "core")
    placed = (
        P(rows, heads),
        P(rows, None),
        P(rows, None),
        P(rows, heads),
        P(rows, heads),
        P(),
        P(),
    )
    return jax.shard_map(
        shards,
        mesh=grid,
        in_specs=placed,
        out_specs=(P(rows, heads), P(rows, None), P(rows, None)),
        check_vma=False,
    )
```
